32 devices in a mesh: sta: 8 (over z, y), tpl: 4 (over x, core).
Axes of the slice: x: 2, y: 2, z: 4, core: 2. Of those that a mesh axis runs over, the one named last changes fastest.
Arguments:
- waveform: float32 [16, 1536], P('sta', 'tpl'), may hold values from -6 to 6
- fir_taps: float32 [64], replicated, may hold values from -0.75 to 0.75
- templates: bfloat16 [512, 16, 1024], P('tpl', 'sta'), may hold values from -6 to 6
- presence: int32 [512, 16], P('tpl', 'sta'), may hold values from 0 to 1
- moveout: int32 [512, 16], P('tpl', 'sta'), may hold values from 0 to 128
Outputs:
- network_stack: float32 [4, 128, 384], P('tpl', 'sta')
The draws below stay inside these ranges and needn't reach their ends.
All inputs are finite; a program needn't handle non-finite values.
Results may differ from the reference program's by a relative error of at most 0.0029.
Values may be sent and summed in bfloat16 or wider, within the bound.
No kernel may reach another device: no remote copies, remote signals or barrier semaphores. Data moves between devices by JAX's collectives and lax.ppermute only.
A program may use at most 64 MiB of HBM per device.

```python
import jax
import jax.numpy as jnp
from jax import lax

TPL = 512
L = 1024
TAPS = 64
BLK = 128
SHIFT_MOST = 128
STA = 16
NS = 1536
TPL_BLOCK = 128
GROUPS = 4


def draw_presence(key, part):
    key_rate, key_bits = jax.random.split(key)
    levels = jax.random.randint(key_rate, (TPL, 1), 2, 10)
    coin_flips = jax.random.randint(key_bits, (TPL, STA), 0, 10)
    return (coin_flips < levels).astype(jnp.int32)


def with_ends(array, key, least, high):
    shape = array.shape
    index_at = [jax.random.randint(jax.random.fold_in(key, axis), (), 0, shape[axis]) for axis in range(len(shape))]
    array = array.at[tuple(index_at)].set(least)
    longest = shape.index(max(shape))
    index_at[longest] = (index_at[longest] + 1) % shape[longest]
    return array.at[tuple(index_at)].set(high)


def level_of(own_key, shape, shards, low, high):
    loudness, own = 1.0, jax.random.fold_in(own_key, 6)
    for dim, parts in shards:
        steps = jnp.exp(jax.random.uniform(jax.random.fold_in(own, dim), (parts,), jnp.float32, low / len(shards), high / len(shards)))
        loudness = loudness * jnp.repeat(steps, shape[dim] // parts).reshape([-1 if axis == dim else 1 for axis in range(len(shape))])
    return loudness


def centred(stream_key, extent, deviation, bound, cuts=(), held_as=jnp.bfloat16):
    values = jax.random.normal(stream_key, extent, jnp.float32) * deviation
    if len(cuts) > 0:
        values = level_of(stream_key, extent, cuts, -0.22, 0.18) * values
    return jnp.clip(values, min=-bound, max=bound).astype(held_as)


def setup_inputs(seed: int = 0) -> dict:
    keys = jax.random.split(jax.random.key(seed), 6)
    return {
        "waveform": centred(keys[0], (STA, NS), 1.0, 6.0, ((0, 8), (1, 4)), jnp.float32),
        "fir_taps": centred(keys[1], (TAPS,), TAPS ** -0.5, 0.75, (), jnp.float32),
        "templates": centred(keys[2], (TPL, STA, L), 1.0, 6.0, ((0, 4), (1, 8))),
        "presence": draw_presence(jax.random.fold_in(keys[5], 71), 0),
        "moveout": with_ends(jax.random.randint(keys[4], (TPL, STA), 0, SHIFT_MOST + 1), jax.random.fold_in(keys[4], 1), 0, SHIFT_MOST).astype(jnp.int32),
    }


epsilon = 1e-06

def fir_apply(extended, coeffs):
    result = lax.conv_general_dilated(extended[:, None, :], coeffs[::-1][None, None, :], (1,), 'VALID', precision=lax.Precision.HIGHEST)
    return result[:, 0, :]

def hankel(samples):
    leading = samples.shape[:-1]
    row_total = samples.shape[-1] // BLK
    row_blocks = samples.reshape(leading + (row_total, BLK))
    windows = jnp.concatenate([row_blocks[..., :-1, :], row_blocks[..., 1:, :]], axis=-1)
    tiled_win = jnp.tile(windows, (1,) * (windows.ndim - 1) + (BLK + 1,))
    flat_win = tiled_win[..., :BLK * (2 * BLK + 1)]
    return flat_win.reshape(windows.shape[:-1] + (BLK, 2 * BLK + 1))[..., :BLK]

def reference(waveform, fir_taps, templates, presence, moveout):
    extended = jnp.pad(waveform, ((0, 0), (TAPS - 1, 0)))
    filtered = fir_apply(extended, fir_taps).astype(jnp.bfloat16)
    corr_len = NS - L
    out_len = corr_len - SHIFT_MOST
    time_blocks = corr_len // BLK
    values = filtered.astype(jnp.float32)
    prefix = jnp.concatenate([jnp.zeros((STA, 1), jnp.float32), jnp.cumsum(values * values, axis=1)], axis=1)
    energy = prefix[:, L:L + corr_len] - prefix[:, :corr_len]

    def station(stack_sum, station_id):
        series = lax.dynamic_index_in_dim(filtered, station_id, 0, keepdims=False)
        hankel_rows = hankel(series).astype(jnp.float32)
        templ_rows = lax.dynamic_index_in_dim(templates, station_id, 1, keepdims=False)
        templ_split = templ_rows.astype(jnp.float32).reshape(TPL, L // BLK, BLK)
        products = jnp.zeros((TPL, time_blocks, BLK), jnp.float32)
        for offset in range(L // BLK):
            products = products + jnp.einsum('kb,cbd->kcd', templ_split[:, offset], hankel_rows[offset:offset + time_blocks], precision=lax.Precision.HIGHEST)
        products = products.reshape(TPL, corr_len)
        templ_norm = jnp.sqrt(lax.optimization_barrier(jnp.sum(templ_rows.astype(jnp.float32) ** 2, axis=-1)) + epsilon)
        station_energy = lax.dynamic_index_in_dim(energy, station_id, 0, keepdims=False)
        correlation = products / (templ_norm[:, None] * jnp.sqrt(station_energy)[None, :])
        shifts = lax.dynamic_index_in_dim(moveout, station_id, 1, keepdims=False).astype(jnp.int32)
        weights = lax.dynamic_index_in_dim(presence, station_id, 1, keepdims=False).astype(jnp.float32)
        aligned = jax.vmap(lambda series_row, offset_value: lax.dynamic_slice_in_dim(series_row, offset_value, out_len))(correlation, shifts)
        return (stack_sum + weights[:, None] * aligned, None)
    stack_sum, _ = lax.scan(station, jnp.zeros((TPL, out_len), jnp.float32), jnp.arange(STA, dtype=jnp.int32))
    return stack_sum.reshape(GROUPS, TPL_BLOCK, out_len)
```

```python
import functools

import jax
import jax.numpy as jnp
from jax import lax
from jax.experimental import pallas as pl
from jax.experimental.pallas import tpu as pltpu
from jax.sharding import PartitionSpec as P

SHIFT_MOST = 128
LANES = 128
epsilon = 1e-06


def lane_gather(values, index):
    return jnp.take_along_axis(values, index, axis=1, mode="promise_in_bounds")


def prep_kernel(templ_ref, presence_ref, moveout_ref, rows_ref, scale_ref, shift_ref):
    stations, block_rows, _ = rows_ref.shape
    for s in range(stations):
        rows = templ_ref[:, s, :]
        rows_ref[s] = rows
        wide = rows.astype(jnp.float32)
        norm = jnp.sqrt(jnp.sum(wide * wide, axis=1, keepdims=True) + epsilon)
        used = jnp.broadcast_to(presence_ref[s : s + 1, :].astype(jnp.float32), (LANES, block_rows)).T
        scale_ref[s] = used / norm
        shift_ref[s] = jnp.broadcast_to(moveout_ref[s : s + 1, :], (LANES, block_rows)).T


def main_kernel(wave_ref, taps_ref, rows_ref, scale_ref, shift_ref, out_ref, hankel_ref):
    stations, block_rows, templ_len = rows_ref.shape
    taps = taps_ref.shape[0]
    samples = wave_ref.shape[1]
    out_len = out_ref.shape[1]
    corr_len = out_len + SHIFT_MOST
    columns = samples // LANES
    lane = lax.broadcasted_iota(jnp.int32, (LANES, LANES), 1)
    row = lax.broadcasted_iota(jnp.int32, (LANES, LANES), 0)
    ahead = lane + row
    ahead_index, ahead_wraps = ahead & (LANES - 1), ahead >= LANES
    back = (lane - row)[:taps]
    back_index, back_wraps = back & (LANES - 1), back < 0
    coeffs = taps_ref[...]
    total = None
    for s in range(stations):
        series = []
        before = jnp.zeros((taps, LANES), jnp.float32)
        for c in range(columns):
            piece = jnp.broadcast_to(wave_ref[s : s + 1, c * LANES : (c + 1) * LANES], (taps, LANES))
            moved = lane_gather(piece, back_index)
            series.append(jnp.sum(coeffs * jnp.where(back_wraps, before, moved), axis=0, keepdims=True))
            before = moved
        squares = []
        prior = None
        for c in range(columns):
            rounded = series[c].astype(jnp.bfloat16).astype(jnp.float32)
            moved = lane_gather(jnp.broadcast_to(rounded, (LANES, LANES)), ahead_index)
            if prior is not None:
                joined = jnp.where(ahead_wraps, moved, prior)
                hankel_ref[s, :, (c - 1) * LANES : c * LANES] = joined.astype(jnp.bfloat16)
                squares.append(jnp.sum(joined * joined, axis=0, keepdims=True))
            prior = moved
        lags = templ_len // LANES
        energy = []
        for t in range(corr_len // LANES):
            part = squares[t]
            for j in range(1, lags):
                part = part + squares[t + j]
            energy.append(part)
        inverse = lax.rsqrt(jnp.concatenate(energy, axis=1))
        raw = None
        for j in range(0, lags, 2):
            window = jnp.concatenate(
                [hankel_ref[s, :, (j + h) * LANES : (j + h) * LANES + corr_len] for h in range(2)], axis=0
            )
            part = jnp.dot(
                rows_ref[s, :, j * LANES : (j + 2) * LANES], window, preferred_element_type=jnp.float32
            )
            raw = part if raw is None else raw + part
        correlation = raw * inverse
        moved_lane = lane[:block_rows] + shift_ref[s]
        index, wraps = moved_lane & (LANES - 1), moved_lane >= LANES
        moved = [
            lane_gather(correlation[:, c * LANES : (c + 1) * LANES], index) for c in range(corr_len // LANES)
        ]
        scale = scale_ref[s]
        aligned = [scale * jnp.where(wraps, moved[c + 1], moved[c]) for c in range(out_len // LANES)]
        total = aligned if total is None else [a + b for a, b in zip(total, aligned)]
    for c, part in enumerate(total):
        out_ref[:, c * LANES : (c + 1) * LANES] = part


def shards(waveform, fir_taps, templates, presence, moveout):
    block_rows, stations, templ_len = templates.shape
    owners = lax.axis_size("sta")
    me = lax.axis_index("sta")
    vmem = pl.BlockSpec(memory_space=pltpu.VMEM)
    rows, scale, shift = pl.pallas_call(
        prep_kernel,
        out_shape=(
            jax.ShapeDtypeStruct((stations, block_rows, templ_len), jnp.bfloat16),
            jax.ShapeDtypeStruct((stations, block_rows, LANES), jnp.float32),
            jax.ShapeDtypeStruct((stations, block_rows, LANES), jnp.int32),
        ),
        in_specs=[vmem] * 3,
        out_specs=(vmem,) * 3,
    )(templates, presence.T, moveout.T)
    wave = lax.all_gather(waveform, "tpl", axis=1, tiled=True)
    samples = wave.shape[1]
    out_len = samples - templ_len - SHIFT_MOST
    stack = pl.pallas_call(
        main_kernel,
        out_shape=jax.ShapeDtypeStruct((block_rows, out_len), jnp.float32),
        in_specs=[vmem] * 5,
        out_specs=vmem,
        scratch_shapes=[pltpu.VMEM((stations, LANES, samples), jnp.bfloat16)],
    )(wave, fir_taps[:, None], rows, scale, shift)
    stack = stack.reshape(owners, block_rows // owners, out_len)
    bit = 1
    while bit < owners:
        half = stack.shape[0] // 2
        pairs = stack.reshape(half, 2, -1, out_len)
        side = (me // bit) % 2
        keep = lax.dynamic_index_in_dim(pairs, side, 1, keepdims=False)
        send = lax.dynamic_index_in_dim(pairs, 1 - side, 1, keepdims=False).astype(jnp.bfloat16)
        got = lax.ppermute(send, "sta", [(i, i ^ bit) for i in range(owners)])
        stack = keep + got.astype(jnp.float32)
        bit *= 2
    return stack.reshape(1, block_rows // owners, out_len)


def solution(mesh):
    placed = (P("sta", "tpl"), P(), P("tpl", "sta", None), P("tpl", "sta"), P("tpl", "sta"))
    return jax.shard_map(
        shards, mesh=mesh, in_specs=placed, out_specs=P("tpl", "sta", None), check_vma=False
    )
```

```python
import functools

import jax
import jax.numpy as jnp
from jax import lax
from jax.experimental import pallas as pl
from jax.experimental.pallas import tpu as pltpu
from jax.sharding import PartitionSpec as P

SHIFT_MOST = 128
LANES = 128
CHUNKS = 4
epsilon = 1e-06


def lane_gather(values, index):
    return jnp.take_along_axis(values, index, axis=1, mode="promise_in_bounds")


def as_column(row):
    return jnp.broadcast_to(row, (LANES, row.shape[1])).T


def rows_kernel(templ_hbm, rows_ref, norm_ref, templ_ref, sems):
    groups, _, owned, stations, _ = templ_ref.shape
    per = groups // CHUNKS if groups % CHUNKS == 0 else groups
    starts = range(0, groups, per)
    chunks = [
        pltpu.make_async_copy(templ_hbm.at[pl.ds(g, per)], templ_ref.at[pl.ds(g, per)], sems.at[g // per])
        for g in starts
    ]
    for copy in chunks:
        copy.start()
    for copy, g in zip(chunks, starts):
        copy.wait()
        at = g * owned
        for s in range(stations):
            for b in range(2):
                rows = templ_ref[g : g + per, b, :, s, :].reshape(per * owned, -1)
                rows_ref[s, b, at : at + per * owned] = rows
                wide = rows.astype(jnp.float32)
                total = jnp.sum(wide * wide, axis=1, keepdims=True)
                norm_ref[s, b, at : at + per * owned] = jnp.broadcast_to(
                    lax.rsqrt(total + epsilon), (per * owned, LANES)
                )


def columns_kernel(owners, wave_in, taps_ref, presence_ref, moveout_ref, wave_ref, coeffs_ref, used_ref, shift_ref):
    stations, _, half_rows, _ = used_ref.shape
    owned = half_rows * 2 // owners
    wave_ref[...] = wave_in[...]
    coeffs_ref[...] = as_column(taps_ref[...])
    place = lax.broadcasted_iota(jnp.int32, (LANES, half_rows * 2), 1)
    half, rest = place // half_rows, place % half_rows
    old = (rest // owned * 2 + half) * owned + rest % owned
    for s in range(stations):
        shift = lane_gather(jnp.broadcast_to(moveout_ref[s : s + 1, :], old.shape), old)
        shift_ref[s] = shift.T.reshape(shift_ref.shape[1:])
        used = lane_gather(jnp.broadcast_to(presence_ref[s : s + 1, :], old.shape), old)
        used_ref[s] = used.astype(jnp.float32).T.reshape(used_ref.shape[1:])


def correlate(rows_of, scale_of, shift_of, window_of, inverse_of, stations, templ_len, out_len):
    total = None
    for s in range(stations):
        raw = None
        for j in range(0, templ_len // LANES, 2):
            part = jnp.dot(rows_of(s, j), window_of(s, j), preferred_element_type=jnp.float32)
            raw = part if raw is None else raw + part
        correlation = raw * inverse_of(s)
        shift = shift_of(s)
        moved_lane = lax.broadcasted_iota(jnp.int32, shift.shape, 1) + shift
        index, wraps = moved_lane & (LANES - 1), moved_lane >= LANES
        moved = [
            lane_gather(correlation[:, at : at + LANES], index) for at in range(0, out_len + SHIFT_MOST, LANES)
        ]
        scale = scale_of(s)
        aligned = [scale * jnp.where(wraps, moved[c + 1], moved[c]) for c in range(out_len // LANES)]
        total = aligned if total is None else [a + b for a, b in zip(total, aligned)]
    return total


def half_of(half, rows_ref, norm_ref, used_ref, shift_ref, hankel_ref, inverse_ref, out_ref):
    stations, _, _, templ_len = rows_ref.shape
    out_len = out_ref.shape[2]
    corr_len = out_len + SHIFT_MOST

    def window(s, j):
        at = j * LANES
        return jnp.concatenate(
            [hankel_ref[s, :, at : at + corr_len], hankel_ref[s, :, at + LANES : at + LANES + corr_len]], axis=0
        )

    total = correlate(
        lambda s, j: rows_ref[s, half, :, j * LANES : (j + 2) * LANES],
        lambda s: norm_ref[s, half] * used_ref[s, half],
        lambda s: shift_ref[s, half],
        window,
        lambda s: inverse_ref[s : s + 1, :],
        stations, templ_len, out_len,
    )
    for c, part in enumerate(total):
        out_ref[:, :, c * LANES : (c + 1) * LANES] = part.astype(out_ref.dtype).reshape(
            out_ref.shape[0], out_ref.shape[1], LANES
        )


def send_kernel(*refs):
    *segment_refs, coeffs_ref, rows_ref, norm_ref, used_ref, shift_ref, send_ref, hankel_ref, inverse_ref, wave_ref = refs
    stations, templ_len = rows_ref.shape[0], rows_ref.shape[3]
    segments = len(segment_refs)
    seg_len = segment_refs[0].shape[1]
    taps = coeffs_ref.shape[0]
    corr_len = inverse_ref.shape[1]
    columns = segments * seg_len // LANES
    tpl = lax.axis_index("tpl")
    for distance, segment_ref in enumerate(segment_refs):
        wave_ref[tpl ^ distance] = segment_ref[...]
    lane = lax.broadcasted_iota(jnp.int32, (LANES, LANES), 1)
    row = lax.broadcasted_iota(jnp.int32, (LANES, LANES), 0)
    ahead = lane + row
    ahead_index, ahead_wraps = ahead & (LANES - 1), ahead >= LANES
    back = (lane - row)[:taps]
    back_index, back_wraps = back & (LANES - 1), back < 0
    coeffs = coeffs_ref[...]
    for s in range(stations):
        series = []
        before = jnp.zeros((taps, LANES), jnp.float32)
        for c in range(columns):
            at = c * LANES
            piece = wave_ref[at // seg_len, s : s + 1, at % seg_len : at % seg_len + LANES]
            moved = lane_gather(jnp.broadcast_to(piece, (taps, LANES)), back_index)
            series.append(jnp.sum(coeffs * jnp.where(back_wraps, before, moved), axis=0, keepdims=True))
            before = moved
        squares = []
        prior = None
        for c in range(columns):
            rounded = series[c].astype(jnp.bfloat16).astype(jnp.float32)
            moved = lane_gather(jnp.broadcast_to(rounded, (LANES, LANES)), ahead_index)
            if prior is not None:
                joined = jnp.where(ahead_wraps, moved, prior)
                hankel_ref[s, :, (c - 1) * LANES : c * LANES] = joined.astype(jnp.bfloat16)
                squares.append(jnp.sum(joined * joined, axis=0, keepdims=True))
            prior = moved
        for t in range(corr_len // LANES):
            part = squares[t]
            for j in range(1, templ_len // LANES):
                part = part + squares[t + j]
            inverse_ref[s : s + 1, t * LANES : (t + 1) * LANES] = lax.rsqrt(part)
    half_of(1 - (lax.axis_index("sta") & 1), rows_ref, norm_ref, used_ref, shift_ref, hankel_ref, inverse_ref, send_ref)


def keep_kernel(rows_ref, norm_ref, used_ref, shift_ref, hankel_ref, inverse_ref, keep_ref):
    half_of(lax.axis_index("sta") & 1, rows_ref, norm_ref, used_ref, shift_ref, hankel_ref, inverse_ref, keep_ref)


def flip(value, axis, bit):
    return lax.ppermute(value, axis, [(i, i ^ bit) for i in range(lax.axis_size(axis))])


def shards(waveform, fir_taps, templates, presence, moveout):
    block_rows, stations, templ_len = templates.shape
    owners, segments = lax.axis_size("sta"), lax.axis_size("tpl")
    sta = lax.axis_index("sta")
    samples = segments * waveform.shape[1]
    corr_len = samples - templ_len
    out_len = corr_len - SHIFT_MOST
    owned = block_rows // owners
    half_rows = block_rows // 2
    vmem = pl.BlockSpec(memory_space=pltpu.VMEM)
    hbm = pl.BlockSpec(memory_space=pltpu.HBM)
    params = pltpu.CompilerParams(vmem_limit_bytes=16 * 1024 * 1024)
    prep_params = pltpu.CompilerParams(vmem_limit_bytes=53 * 1024 * 1024)

    def cost(flops):
        return pl.CostEstimate(flops=flops, bytes_accessed=1 << 20, transcendentals=0)

    paired = (owners // 2, 2, owned, stations, templ_len)
    rows, norm = pl.pallas_call(
        rows_kernel,
        out_shape=(
            jax.ShapeDtypeStruct((stations, 2, half_rows, templ_len), jnp.bfloat16),
            jax.ShapeDtypeStruct((stations, 2, half_rows, LANES), jnp.float32),
        ),
        in_specs=[hbm],
        out_specs=(vmem,) * 2,
        scratch_shapes=[pltpu.VMEM(paired, jnp.bfloat16), pltpu.SemaphoreType.DMA((CHUNKS,))],
        compiler_params=prep_params,
        cost_estimate=cost(1 << 20),
        name="template_rows",
    )(templates.reshape(paired))
    own, coeffs, used, shift = pl.pallas_call(
        functools.partial(columns_kernel, owners),
        out_shape=(
            jax.ShapeDtypeStruct(waveform.shape, jnp.float32),
            jax.ShapeDtypeStruct((fir_taps.shape[0], LANES), jnp.float32),
            jax.ShapeDtypeStruct((stations, 2, half_rows, LANES), jnp.float32),
            jax.ShapeDtypeStruct((stations, 2, half_rows, LANES), jnp.int32),
        ),
        in_specs=[vmem] * 4,
        out_specs=(vmem,) * 4,
        compiler_params=params,
        cost_estimate=cost(1 << 20),
        name="columns",
    )(waveform, fir_taps[None, :], presence.T, moveout.T)
    bit = segments // 2
    sent = {0: waveform}
    while bit >= 1:
        for d, piece in list(sent.items()):
            sent[d ^ bit] = flip(piece, "tpl", bit)
        if bit == segments // 2:
            sent[bit], rows, norm = lax.optimization_barrier((sent[bit], rows, norm))
        bit //= 2
    sent[0] = own
    send, hankel, inverse = pl.pallas_call(
        send_kernel,
        out_shape=(
            jax.ShapeDtypeStruct((owners // 2, owned, out_len), jnp.bfloat16),
            jax.ShapeDtypeStruct((stations, LANES, samples), jnp.bfloat16),
            jax.ShapeDtypeStruct((stations, corr_len), jnp.float32),
        ),
        in_specs=[vmem] * (segments + 5),
        out_specs=(vmem,) * 3,
        scratch_shapes=[pltpu.VMEM((segments,) + waveform.shape, jnp.float32)],
        compiler_params=params,
        cost_estimate=cost(1 << 20),
        name="send_half",
    )(*[sent[d] for d in range(segments)], coeffs, rows, norm, used, shift)
    keep = pl.pallas_call(
        keep_kernel,
        out_shape=jax.ShapeDtypeStruct((owners // 2, owned, out_len), jnp.float32),
        in_specs=[vmem] * 6,
        out_specs=vmem,
        compiler_params=params,
        cost_estimate=cost(1 << 20),
        name="keep_half",
    )(rows, norm, used, shift, hankel, inverse)
    stack = keep
    bit = 1
    while True:
        stack = stack + flip(send, "sta", bit).astype(jnp.float32)
        bit *= 2
        if bit >= owners:
            break
        pairs = stack.reshape(stack.shape[0] // 2, 2, owned, out_len)
        side = (sta // bit) % 2
        stack = lax.dynamic_index_in_dim(pairs, side, 1, keepdims=False)
        send = lax.dynamic_index_in_dim(pairs, 1 - side, 1, keepdims=False).astype(jnp.bfloat16)
    return stack


def solution(mesh):
    placed = (P("sta", "tpl"), P(), P("tpl", "sta", None), P("tpl", "sta"), P("tpl", "sta"))
    return jax.shard_map(
        shards, mesh=mesh, in_specs=placed, out_specs=P("tpl", "sta", None), check_vma=False
    )
```

```python
import functools

import jax
import jax.numpy as jnp
from jax import lax
from jax.experimental import pallas as pl
from jax.experimental.pallas import tpu as pltpu
from jax.sharding import PartitionSpec as P

SHIFT_MOST = 128
LANES = 128
PAIR = 2 * LANES
epsilon = 1e-06


def lane_gather(values, index):
    return jnp.take_along_axis(values, index, axis=1, mode="promise_in_bounds")


def as_column(row):
    return jnp.broadcast_to(row, (LANES, row.shape[1])).T


def columns_kernel(owners, wave_in, taps_in, presence_ref, moveout_ref, wave_ref, toeplitz_ref, used_ref, shift_ref, row_ref):
    stations, _, half_rows, _ = used_ref.shape
    owned = half_rows * 2 // owners
    taps = taps_in.shape[1]
    wave_ref[...] = wave_in[...]
    row_ref[...] = jnp.zeros_like(row_ref)
    row_ref[0:1, 0:taps] = taps_in[...]
    sample = lax.broadcasted_iota(jnp.int32, (PAIR, LANES), 0)
    lane = lax.broadcasted_iota(jnp.int32, (PAIR, LANES), 1)
    tap = PAIR - 1 - lane - sample
    picked = lane_gather(jnp.broadcast_to(row_ref[0:1, :], (PAIR, LANES)), tap & (LANES - 1))
    toeplitz_ref[...] = jnp.where((tap >= 0) & (tap < taps), picked, 0.0)
    place = lax.broadcasted_iota(jnp.int32, (LANES, half_rows * 2), 1)
    half, rest = place // half_rows, place % half_rows
    old = (rest // owned * 2 + half) * owned + rest % owned
    for s in range(stations):
        shift = lane_gather(jnp.broadcast_to(moveout_ref[s : s + 1, :], old.shape), old)
        shift_ref[s] = shift.T.reshape(shift_ref.shape[1:])
        used = lane_gather(jnp.broadcast_to(presence_ref[s : s + 1, :], old.shape), old)
        used_ref[s] = used.astype(jnp.float32).T.reshape(used_ref.shape[1:])


def stack_half(half, rows_ref, used_ref, shift_ref, hankel_ref, inverse_ref, out_ref):
    stations, groups, _, owned, templ_len = rows_ref.shape
    half_rows = groups * owned
    corr_len = inverse_ref.shape[1]
    out_len = out_ref.shape[2]
    lag_pairs, time_pairs = templ_len // PAIR, corr_len // PAIR
    total = None
    for s in range(stations):
        rows = rows_ref[s, :, half].reshape(half_rows, templ_len)
        raw = [None] * time_pairs
        for offset in range(1, lag_pairs + time_pairs):
            uses = [(j, offset - lag_pairs + j) for j in range(lag_pairs) if 0 <= offset - lag_pairs + j < time_pairs]
            at = offset * PAIR
            window = jnp.concatenate(
                [hankel_ref[s, :, at : at + PAIR], hankel_ref[s, :, at - LANES : at - LANES + PAIR]], axis=0
            )
            left = jnp.concatenate([rows[:, j * PAIR : (j + 1) * PAIR] for j, _ in uses], axis=0)
            product = jnp.dot(left, window, preferred_element_type=jnp.float32)
            for k, (_, t) in enumerate(uses):
                part = product[k * half_rows : (k + 1) * half_rows]
                raw[t] = part if raw[t] is None else raw[t] + part
        correlation = jnp.concatenate(raw, axis=1) * inverse_ref[s : s + 1, :]
        wide = rows.astype(jnp.float32)
        norm = lax.rsqrt(jnp.sum(wide * wide, axis=1, keepdims=True) + epsilon)
        shift = shift_ref[s, half]
        place = PAIR - 1 - lax.broadcasted_iota(jnp.int32, shift.shape, 1) - shift
        index, later = place & (LANES - 1), place >= LANES
        moved = [lane_gather(correlation[:, at : at + LANES], index) for at in range(0, corr_len, LANES)]
        last = corr_len // LANES - 1
        scale = norm * used_ref[s, half]
        aligned = [scale * jnp.where(later, moved[last - c], moved[last - 1 - c]) for c in range(out_len // LANES)]
        total = aligned if total is None else [a + b for a, b in zip(total, aligned)]
    for c, part in enumerate(total):
        out_ref[:, :, c * LANES : (c + 1) * LANES] = part.astype(out_ref.dtype).reshape(groups, owned, LANES)


def send_kernel(*refs):
    *segment_refs, toeplitz_ref, rows_ref, used_ref, shift_ref = refs[:-7]
    send_ref, hankel_ref, inverse_ref, wave_ref, series_ref, sums_of_ref, sums_ref = refs[-7:]
    stations, templ_len = rows_ref.shape[0], rows_ref.shape[-1]
    corr_len = inverse_ref.shape[1]
    seg_len = segment_refs[0].shape[1]
    blocks = len(segment_refs) * seg_len // LANES
    lags, times = templ_len // LANES, corr_len // LANES
    tpl = lax.axis_index("tpl")
    for distance, segment_ref in enumerate(segment_refs):
        wave_ref[tpl ^ distance] = segment_ref[...]
    places = [(c * LANES // seg_len, c * LANES % seg_len) for c in range(blocks)]
    block = jnp.concatenate([wave_ref[g, :, at : at + LANES] for g, at in places], axis=0)
    before = jnp.concatenate([jnp.zeros((stations, LANES), jnp.float32), block[:-stations]], axis=0)
    filtered = jnp.dot(
        jnp.concatenate([before, block], axis=1),
        toeplitz_ref[...],
        precision=lax.Precision.HIGHEST,
        preferred_element_type=jnp.float32,
    )
    series = filtered.astype(jnp.bfloat16).astype(jnp.float32)
    series_ref[...] = series
    row = lax.broadcasted_iota(jnp.int32, (LANES, LANES), 0)
    lane = lax.broadcasted_iota(jnp.int32, (LANES, LANES), 1)
    one = jnp.ones((LANES, LANES), jnp.float32)
    sums_of_ref[...] = jnp.concatenate(
        [jnp.where(row <= lane, one, 0.0), jnp.where(row > lane, one, 0.0), one], axis=1
    ).astype(jnp.bfloat16)
    squares = series * series
    high = squares.astype(jnp.bfloat16)
    low = (squares - high.astype(jnp.float32)).astype(jnp.bfloat16)
    sums_ref[...] = jnp.dot(high, sums_of_ref[...], preferred_element_type=jnp.float32) + jnp.dot(
        low, sums_of_ref[...], preferred_element_type=jnp.float32
    )

    def sums(c, kind):
        return sums_ref[c * stations : (c + 1) * stations, kind * LANES : (kind + 1) * LANES]

    for t in range(times):
        energy = sums(t, 0) + sums(t + lags, 1)
        for c in range(t + 1, t + lags):
            energy = energy + sums(c, 2)
        at = (times - 1 - t) * LANES
        inverse_ref[:, at : at + LANES] = lax.rsqrt(energy)
    for s in range(stations):
        whole = jnp.concatenate(
            [series_ref[c * stations + s : c * stations + s + 1, :] for c in reversed(range(blocks))], axis=1
        )
        ahead = pltpu.roll(
            jnp.broadcast_to(whole, (LANES, blocks * LANES)), 0, 1, stride=1, stride_axis=0
        )
        for c in range(1, blocks):
            hankel_ref[s, :, c * LANES : (c + 1) * LANES] = ahead[:, c * LANES : (c + 1) * LANES].astype(jnp.bfloat16)
    stack_half(1 - (lax.axis_index("sta") & 1), rows_ref, used_ref, shift_ref, hankel_ref, inverse_ref, send_ref)


def keep_kernel(rows_ref, used_ref, shift_ref, hankel_ref, inverse_ref, keep_ref):
    stack_half(lax.axis_index("sta") & 1, rows_ref, used_ref, shift_ref, hankel_ref, inverse_ref, keep_ref)


def flip(value, axis, mask):
    return lax.ppermute(value, axis, [(i, i ^ mask) for i in range(lax.axis_size(axis))])


def shards(waveform, fir_taps, templates, presence, moveout):
    block_rows, stations, templ_len = templates.shape
    owners, segments = lax.axis_size("sta"), lax.axis_size("tpl")
    sta = lax.axis_index("sta")
    samples = segments * waveform.shape[1]
    corr_len = samples - templ_len
    out_len = corr_len - SHIFT_MOST
    owned = block_rows // owners
    half_rows = block_rows // 2
    vmem = pl.BlockSpec(memory_space=pltpu.VMEM)
    options = dict(
        compiler_params=pltpu.CompilerParams(vmem_limit_bytes=16 * 1024 * 1024),
        cost_estimate=pl.CostEstimate(flops=1 << 20, bytes_accessed=1 << 20, transcendentals=0),
    )
    rows = templates.transpose(1, 0, 2).reshape(stations, owners // 2, 2, owned, templ_len)
    own, toeplitz, used, shift = pl.pallas_call(
        functools.partial(columns_kernel, owners),
        out_shape=(
            jax.ShapeDtypeStruct(waveform.shape, jnp.float32),
            jax.ShapeDtypeStruct((PAIR, LANES), jnp.float32),
            jax.ShapeDtypeStruct((stations, 2, half_rows, LANES), jnp.float32),
            jax.ShapeDtypeStruct((stations, 2, half_rows, LANES), jnp.int32),
        ),
        in_specs=[vmem] * 4,
        out_specs=(vmem,) * 4,
        scratch_shapes=[pltpu.VMEM((8, LANES), jnp.float32)],
        name="columns",
        **options,
    )(waveform, fir_taps[None, :], presence.T, moveout.T)
    sent = {0: waveform}
    bit = segments // 2
    while bit >= 1:
        mask = bit | 1
        for d, piece in list(sent.items()):
            sent[d ^ mask] = flip(piece, "tpl", mask)
        if bit == segments // 2:
            sent[mask], rows = lax.optimization_barrier((sent[mask], rows))
        bit //= 2
    sent[0] = own
    send, hankel, inverse = pl.pallas_call(
        send_kernel,
        out_shape=(
            jax.ShapeDtypeStruct((owners // 2, owned, out_len), jnp.bfloat16),
            jax.ShapeDtypeStruct((stations, LANES, samples), jnp.bfloat16),
            jax.ShapeDtypeStruct((stations, corr_len), jnp.float32),
        ),
        in_specs=[vmem] * (segments + 4),
        out_specs=(vmem,) * 3,
        scratch_shapes=[
            pltpu.VMEM((segments,) + waveform.shape, jnp.float32),
            pltpu.VMEM((samples // LANES * stations, LANES), jnp.float32),
            pltpu.VMEM((LANES, 3 * LANES), jnp.bfloat16),
            pltpu.VMEM((samples // LANES * stations, 3 * LANES), jnp.float32),
        ],
        name="send_half",
        **options,
    )(*[sent[d] for d in range(segments)], toeplitz, rows, used, shift)
    stack = pl.pallas_call(
        keep_kernel,
        out_shape=jax.ShapeDtypeStruct((owners // 2, owned, out_len), jnp.float32),
        in_specs=[vmem] * 5,
        out_specs=vmem,
        name="keep_half",
        **options,
    )(rows, used, shift, hankel, inverse)
    bit = 1
    while True:
        stack = stack + flip(send, "sta", bit).astype(jnp.float32)
        bit *= 2
        if bit >= owners:
            break
        pairs = stack.reshape(stack.shape[0] // 2, 2, owned, out_len)
        side = (sta // bit) % 2
        stack = lax.dynamic_index_in_dim(pairs, side, 1, keepdims=False)
        send = lax.dynamic_index_in_dim(pairs, 1 - side, 1, keepdims=False).astype(jnp.bfloat16)
    return stack


def solution(mesh):
    placed = (P("sta", "tpl"), P(), P("tpl", "sta", None), P("tpl", "sta"), P("tpl", "sta"))
    return jax.shard_map(
        shards, mesh=mesh, in_specs=placed, out_specs=P("tpl", "sta", None), check_vma=False
    )
```

```python
import functools

import jax
import jax.numpy as jnp
from jax import lax
from jax.experimental import pallas as pl
from jax.experimental.pallas import tpu as pltpu
from jax.sharding import PartitionSpec as P

SHIFT_MOST = 128
LANES = 128
PAIR = 2 * LANES
epsilon = 1e-06


def lane_gather(values, index):
    return jnp.take_along_axis(values, index, axis=1, mode="promise_in_bounds")


def as_column(row):
    return jnp.broadcast_to(row, (LANES, row.shape[1])).T


def columns_kernel(owners, wave_in, taps_in, presence_ref, moveout_ref, wave_ref, toeplitz_ref, used_ref, shift_ref, row_ref):
    stations, parts, part_rows, _ = used_ref.shape
    owned = part_rows * parts // owners
    taps = taps_in.shape[1]
    wave_ref[...] = wave_in[...]
    row_ref[...] = jnp.zeros_like(row_ref)
    row_ref[0:1, 0:taps] = taps_in[...]
    sample = lax.broadcasted_iota(jnp.int32, (PAIR, LANES), 0)
    lane = lax.broadcasted_iota(jnp.int32, (PAIR, LANES), 1)
    tap = PAIR - 1 - lane - sample
    picked = lane_gather(jnp.broadcast_to(row_ref[0:1, :], (PAIR, LANES)), tap & (LANES - 1))
    toeplitz_ref[...] = jnp.where((tap >= 0) & (tap < taps), picked, 0.0)
    place = lax.broadcasted_iota(jnp.int32, (LANES, part_rows * parts), 1)
    part, rest = place // part_rows, place % part_rows
    old = (rest // owned * parts + part) * owned + rest % owned
    for s in range(stations):
        shift = lane_gather(jnp.broadcast_to(moveout_ref[s : s + 1, :], old.shape), old)
        shift_ref[s] = shift.T.reshape(shift_ref.shape[1:])
        used = lane_gather(jnp.broadcast_to(presence_ref[s : s + 1, :], old.shape), old)
        used_ref[s] = used.astype(jnp.float32).T.reshape(used_ref.shape[1:])


def stack_parts(parts, rows_ref, used_ref, shift_ref, hankel_ref, inverse_ref, out_refs):
    stations, groups, _, owned, templ_len = rows_ref.shape
    part_rows = groups * owned
    all_rows = len(parts) * part_rows
    corr_len = inverse_ref.shape[1]
    out_len = out_refs[0].shape[2]
    lag_pairs, time_pairs = templ_len // PAIR, corr_len // PAIR
    total = None
    for s in range(stations):
        rows = jnp.concatenate([rows_ref[s, :, p].reshape(part_rows, templ_len) for p in parts], axis=0)
        raw = [None] * time_pairs
        for offset in range(1, lag_pairs + time_pairs):
            uses = [(j, offset - lag_pairs + j) for j in range(lag_pairs) if 0 <= offset - lag_pairs + j < time_pairs]
            at = offset * PAIR
            window = jnp.concatenate(
                [hankel_ref[s, :, at : at + PAIR], hankel_ref[s, :, at - LANES : at - LANES + PAIR]], axis=0
            )
            left = jnp.concatenate([rows[:, j * PAIR : (j + 1) * PAIR] for j, _ in uses], axis=0)
            product = jnp.dot(left, window, preferred_element_type=jnp.float32)
            for k, (_, t) in enumerate(uses):
                part = product[k * all_rows : (k + 1) * all_rows]
                raw[t] = part if raw[t] is None else raw[t] + part
        correlation = jnp.concatenate(raw, axis=1) * inverse_ref[s : s + 1, :]
        wide = rows.astype(jnp.float32)
        norm = lax.rsqrt(jnp.sum(wide * wide, axis=1, keepdims=True) + epsilon)
        shift = jnp.concatenate([shift_ref[s, p] for p in parts], axis=0)
        place = PAIR - 1 - lax.broadcasted_iota(jnp.int32, shift.shape, 1) - shift
        index, later = place & (LANES - 1), place >= LANES
        moved = [lane_gather(correlation[:, at : at + LANES], index) for at in range(0, corr_len, LANES)]
        last = corr_len // LANES - 1
        scale = norm * jnp.concatenate([used_ref[s, p] for p in parts], axis=0)
        aligned = [scale * jnp.where(later, moved[last - c], moved[last - 1 - c]) for c in range(out_len // LANES)]
        total = aligned if total is None else [a + b for a, b in zip(total, aligned)]
    for k, out_ref in enumerate(out_refs):
        for c, part in enumerate(total):
            piece = part[k * part_rows : (k + 1) * part_rows].astype(out_ref.dtype)
            out_ref[:, :, c * LANES : (c + 1) * LANES] = piece.reshape(groups, owned, LANES)


def send_kernel(segments, *refs):
    segment_refs, (toeplitz_ref, rows_ref, used_ref, shift_ref, *send_refs) = refs[:segments], refs[segments:-6]
    hankel_ref, inverse_ref, wave_ref, series_ref, sums_of_ref, sums_ref = refs[-6:]
    stations, templ_len = rows_ref.shape[0], rows_ref.shape[-1]
    corr_len = inverse_ref.shape[1]
    seg_len = segment_refs[0].shape[1]
    blocks = len(segment_refs) * seg_len // LANES
    lags, times = templ_len // LANES, corr_len // LANES
    tpl = lax.axis_index("tpl")
    for distance, segment_ref in enumerate(segment_refs):
        wave_ref[tpl ^ distance] = segment_ref[...]
    places = [(c * LANES // seg_len, c * LANES % seg_len) for c in range(blocks)]
    block = jnp.concatenate([wave_ref[g, :, at : at + LANES] for g, at in places], axis=0)
    before = jnp.concatenate([jnp.zeros((stations, LANES), jnp.float32), block[:-stations]], axis=0)
    filtered = jnp.dot(
        jnp.concatenate([before, block], axis=1),
        toeplitz_ref[...],
        precision=lax.Precision.HIGHEST,
        preferred_element_type=jnp.float32,
    )
    series = filtered.astype(jnp.bfloat16).astype(jnp.float32)
    series_ref[...] = series
    row = lax.broadcasted_iota(jnp.int32, (LANES, LANES), 0)
    lane = lax.broadcasted_iota(jnp.int32, (LANES, LANES), 1)
    one = jnp.ones((LANES, LANES), jnp.float32)
    sums_of_ref[...] = jnp.concatenate(
        [jnp.where(row <= lane, one, 0.0), jnp.where(row > lane, one, 0.0), one], axis=1
    ).astype(jnp.bfloat16)
    squares = series * series
    high = squares.astype(jnp.bfloat16)
    low = (squares - high.astype(jnp.float32)).astype(jnp.bfloat16)
    sums_ref[...] = jnp.dot(high, sums_of_ref[...], preferred_element_type=jnp.float32) + jnp.dot(
        low, sums_of_ref[...], preferred_element_type=jnp.float32
    )

    def sums(c, kind):
        return sums_ref[c * stations : (c + 1) * stations, kind * LANES : (kind + 1) * LANES]

    for t in range(times):
        energy = sums(t, 0) + sums(t + lags, 1)
        for c in range(t + 1, t + lags):
            energy = energy + sums(c, 2)
        at = (times - 1 - t) * LANES
        inverse_ref[:, at : at + LANES] = lax.rsqrt(energy)
    for s in range(stations):
        whole = jnp.concatenate(
            [series_ref[c * stations + s : c * stations + s + 1, :] for c in reversed(range(blocks))], axis=1
        )
        ahead = pltpu.roll(
            jnp.broadcast_to(whole, (LANES, blocks * LANES)), 0, 1, stride=1, stride_axis=0
        )
        for c in range(1, blocks):
            hankel_ref[s, :, c * LANES : (c + 1) * LANES] = ahead[:, c * LANES : (c + 1) * LANES].astype(jnp.bfloat16)
    me = lax.axis_index("sta") & len(send_refs)
    parts = [me ^ distance for distance in range(1, len(send_refs) + 1)]
    stack_parts(parts, rows_ref, used_ref, shift_ref, hankel_ref, inverse_ref, send_refs)


def keep_kernel(rows_ref, used_ref, shift_ref, hankel_ref, inverse_ref, keep_ref):
    me = lax.axis_index("sta") & (rows_ref.shape[2] - 1)
    stack_parts([me], rows_ref, used_ref, shift_ref, hankel_ref, inverse_ref, [keep_ref])


def flip(value, axis, mask):
    return lax.ppermute(value, axis, [(i, i ^ mask) for i in range(lax.axis_size(axis))])


def shards(waveform, fir_taps, templates, presence, moveout):
    block_rows, stations, templ_len = templates.shape
    owners, segments = lax.axis_size("sta"), lax.axis_size("tpl")
    sta = lax.axis_index("sta")
    samples = segments * waveform.shape[1]
    corr_len = samples - templ_len
    out_len = corr_len - SHIFT_MOST
    owned = block_rows // owners
    parts = min(owners, 4)
    part_rows = block_rows // parts
    vmem = pl.BlockSpec(memory_space=pltpu.VMEM)
    options = dict(
        compiler_params=pltpu.CompilerParams(vmem_limit_bytes=16 * 1024 * 1024),
        cost_estimate=pl.CostEstimate(flops=1 << 20, bytes_accessed=1 << 20, transcendentals=0),
    )
    rows = templates.transpose(1, 0, 2).reshape(stations, owners // parts, parts, owned, templ_len)
    own, toeplitz, used, shift = pl.pallas_call(
        functools.partial(columns_kernel, owners),
        out_shape=(
            jax.ShapeDtypeStruct(waveform.shape, jnp.float32),
            jax.ShapeDtypeStruct((PAIR, LANES), jnp.float32),
            jax.ShapeDtypeStruct((stations, parts, part_rows, LANES), jnp.float32),
            jax.ShapeDtypeStruct((stations, parts, part_rows, LANES), jnp.int32),
        ),
        in_specs=[vmem] * 4,
        out_specs=(vmem,) * 4,
        scratch_shapes=[pltpu.VMEM((8, LANES), jnp.float32)],
        name="columns",
        **options,
    )(waveform, fir_taps[None, :], presence.T, moveout.T)
    sent = {0: waveform}
    bit = segments // 2
    while bit >= 1:
        mask = bit | 1
        for d, piece in list(sent.items()):
            sent[d ^ mask] = flip(piece, "tpl", mask)
        if bit == segments // 2:
            sent[mask], rows = lax.optimization_barrier((sent[mask], rows))
        bit //= 2
    sent[0] = own
    *send, hankel, inverse = pl.pallas_call(
        functools.partial(send_kernel, segments),
        out_shape=(
            *[jax.ShapeDtypeStruct((owners // parts, owned, out_len), jnp.bfloat16)] * (parts - 1),
            jax.ShapeDtypeStruct((stations, LANES, samples), jnp.bfloat16),
            jax.ShapeDtypeStruct((stations, corr_len), jnp.float32),
        ),
        in_specs=[vmem] * (segments + 4),
        out_specs=(vmem,) * (parts + 1),
        scratch_shapes=[
            pltpu.VMEM((segments,) + waveform.shape, jnp.float32),
            pltpu.VMEM((samples // LANES * stations, LANES), jnp.float32),
            pltpu.VMEM((LANES, 3 * LANES), jnp.bfloat16),
            pltpu.VMEM((samples // LANES * stations, 3 * LANES), jnp.float32),
        ],
        name="send_parts",
        **options,
    )(*[sent[d] for d in range(segments)], toeplitz, rows, used, shift)
    stack = pl.pallas_call(
        keep_kernel,
        out_shape=jax.ShapeDtypeStruct((owners // parts, owned, out_len), jnp.float32),
        in_specs=[vmem] * 5,
        out_specs=vmem,
        name="keep_part",
        **options,
    )(rows, used, shift, hankel, inverse)
    for distance in range(1, parts):
        stack = stack + flip(send[distance - 1], "sta", distance).astype(jnp.float32)
    bit = parts
    while bit < owners:
        pairs = stack.reshape(stack.shape[0] // 2, 2, owned, out_len)
        side = (sta // bit) % 2
        stack = lax.dynamic_index_in_dim(pairs, side, 1, keepdims=False)
        other = lax.dynamic_index_in_dim(pairs, 1 - side, 1, keepdims=False).astype(jnp.bfloat16)
        stack = stack + flip(other, "sta", bit).astype(jnp.float32)
        bit *= 2
    return stack


def solution(mesh):
    placed = (P("sta", "tpl"), P(), P("tpl", "sta", None), P("tpl", "sta"), P("tpl", "sta"))
    return jax.shard_map(
        shards, mesh=mesh, in_specs=placed, out_specs=P("tpl", "sta", None), check_vma=False
    )
```

```python
import functools

import jax
import jax.numpy as jnp
from jax import lax
from jax.experimental import pallas as pl
from jax.experimental.pallas import tpu as pltpu
from jax.sharding import PartitionSpec as P

SHIFT_MOST = 128
LANES = 128
PAIR = 2 * LANES
epsilon = 1e-06


def lane_gather(values, index):
    return jnp.take_along_axis(values, index, axis=1, mode="promise_in_bounds")


def as_column(row):
    return jnp.broadcast_to(row, (LANES, row.shape[1])).T


def columns_kernel(owners, wave_in, taps_in, presence_ref, moveout_ref, wave_ref, toeplitz_ref, used_ref, shift_ref, row_ref):
    stations, parts, part_rows, _ = used_ref.shape
    owned = part_rows * parts // owners
    taps = taps_in.shape[1]
    wave_ref[...] = wave_in[...]
    row_ref[...] = jnp.zeros_like(row_ref)
    row_ref[0:1, 0:taps] = taps_in[...]
    sample = lax.broadcasted_iota(jnp.int32, (PAIR, LANES), 0)
    lane = lax.broadcasted_iota(jnp.int32, (PAIR, LANES), 1)
    tap = PAIR - 1 - lane - sample
    picked = lane_gather(jnp.broadcast_to(row_ref[0:1, :], (PAIR, LANES)), tap & (LANES - 1))
    toeplitz_ref[...] = jnp.where((tap >= 0) & (tap < taps), picked, 0.0)
    place = lax.broadcasted_iota(jnp.int32, (LANES, part_rows * parts), 1)
    part, rest = place // part_rows, place % part_rows
    old = (rest // owned * parts + part) * owned + rest % owned
    for s in range(stations):
        shift = lane_gather(jnp.broadcast_to(moveout_ref[s : s + 1, :], old.shape), old)
        shift_ref[s] = shift.T.reshape(shift_ref.shape[1:])
        used = lane_gather(jnp.broadcast_to(presence_ref[s : s + 1, :], old.shape), old)
        used_ref[s] = used.astype(jnp.float32).T.reshape(used_ref.shape[1:])


def stack_parts(parts, rows_ref, used_ref, shift_ref, hankel_ref, inverse_ref, out_refs):
    stations, groups, _, owned, templ_len = rows_ref.shape
    part_rows = groups * owned
    all_rows = len(parts) * part_rows
    corr_len = inverse_ref.shape[1]
    out_len = out_refs[0].shape[2]
    lag_pairs, time_pairs = templ_len // PAIR, corr_len // PAIR
    total = None
    for s in range(stations):
        rows = jnp.concatenate([rows_ref[s, :, p].reshape(part_rows, templ_len) for p in parts], axis=0)
        raw = [None] * time_pairs
        for offset in range(1, lag_pairs + time_pairs):
            uses = [(j, offset - lag_pairs + j) for j in range(lag_pairs) if 0 <= offset - lag_pairs + j < time_pairs]
            at = offset * PAIR
            window = jnp.concatenate(
                [hankel_ref[s, :, at : at + PAIR], hankel_ref[s, :, at - LANES : at - LANES + PAIR]], axis=0
            )
            left = jnp.concatenate([rows[:, j * PAIR : (j + 1) * PAIR] for j, _ in uses], axis=0)
            product = jnp.dot(left, window, preferred_element_type=jnp.float32)
            for k, (_, t) in enumerate(uses):
                part = product[k * all_rows : (k + 1) * all_rows]
                raw[t] = part if raw[t] is None else raw[t] + part
        correlation = jnp.concatenate(raw, axis=1) * inverse_ref[s : s + 1, :]
        wide = rows.astype(jnp.float32)
        norm = lax.rsqrt(jnp.sum(wide * wide, axis=1, keepdims=True) + epsilon)
        shift = jnp.concatenate([shift_ref[s, p] for p in parts], axis=0)
        lane = lax.broadcasted_iota(jnp.int32, shift.shape, 1)
        index = (PAIR - 1 - lane - shift) & (LANES - 1)
        later = lane + shift < LANES
        columns = [correlation[:, at : at + LANES] for at in range(0, corr_len, LANES)]
        last = corr_len // LANES - 1
        scale = norm * jnp.concatenate([used_ref[s, p] for p in parts], axis=0)
        aligned = [
            scale * lane_gather(jnp.where(later, columns[last - c], columns[last - 1 - c]), index)
            for c in range(out_len // LANES)
        ]
        total = aligned if total is None else [a + b for a, b in zip(total, aligned)]
    for k, out_ref in enumerate(out_refs):
        for c, part in enumerate(total):
            piece = part[k * part_rows : (k + 1) * part_rows].astype(out_ref.dtype)
            out_ref[:, :, c * LANES : (c + 1) * LANES] = piece.reshape(groups, owned, LANES)


def send_kernel(segments, *refs):
    segment_refs, (toeplitz_ref, rows_ref, used_ref, shift_ref, *send_refs) = refs[:segments], refs[segments:-6]
    hankel_ref, inverse_ref, wave_ref, series_ref, sums_of_ref, sums_ref = refs[-6:]
    stations, templ_len = rows_ref.shape[0], rows_ref.shape[-1]
    corr_len = inverse_ref.shape[1]
    seg_len = segment_refs[0].shape[1]
    blocks = len(segment_refs) * seg_len // LANES
    lags, times = templ_len // LANES, corr_len // LANES
    tpl = lax.axis_index("tpl")
    for distance, segment_ref in enumerate(segment_refs):
        wave_ref[tpl ^ distance] = segment_ref[...]
    places = [(c * LANES // seg_len, c * LANES % seg_len) for c in range(blocks)]
    block = jnp.concatenate([wave_ref[g, :, at : at + LANES] for g, at in places], axis=0)
    before = jnp.concatenate([jnp.zeros((stations, LANES), jnp.float32), block[:-stations]], axis=0)
    filtered = jnp.dot(
        jnp.concatenate([before, block], axis=1),
        toeplitz_ref[...],
        precision=lax.Precision.HIGHEST,
        preferred_element_type=jnp.float32,
    )
    series = filtered.astype(jnp.bfloat16).astype(jnp.float32)
    series_ref[...] = series
    row = lax.broadcasted_iota(jnp.int32, (LANES, LANES), 0)
    lane = lax.broadcasted_iota(jnp.int32, (LANES, LANES), 1)
    one = jnp.ones((LANES, LANES), jnp.float32)
    sums_of_ref[...] = jnp.concatenate(
        [jnp.where(row <= lane, one, 0.0), jnp.where(row > lane, one, 0.0), one], axis=1
    ).astype(jnp.bfloat16)
    squares = series * series
    high = squares.astype(jnp.bfloat16)
    low = (squares - high.astype(jnp.float32)).astype(jnp.bfloat16)
    sums_ref[...] = jnp.dot(high, sums_of_ref[...], preferred_element_type=jnp.float32) + jnp.dot(
        low, sums_of_ref[...], preferred_element_type=jnp.float32
    )

    def sums(c, kind):
        return sums_ref[c * stations : (c + 1) * stations, kind * LANES : (kind + 1) * LANES]

    for t in range(times):
        energy = sums(t, 0) + sums(t + lags, 1)
        for c in range(t + 1, t + lags):
            energy = energy + sums(c, 2)
        at = (times - 1 - t) * LANES
        inverse_ref[:, at : at + LANES] = lax.rsqrt(energy)
    for s in range(stations):
        whole = jnp.concatenate(
            [series_ref[c * stations + s : c * stations + s + 1, :] for c in reversed(range(blocks))], axis=1
        )
        ahead = pltpu.roll(
            jnp.broadcast_to(whole, (LANES, blocks * LANES)), 0, 1, stride=1, stride_axis=0
        )
        for c in range(1, blocks):
            hankel_ref[s, :, c * LANES : (c + 1) * LANES] = ahead[:, c * LANES : (c + 1) * LANES].astype(jnp.bfloat16)
    me = lax.axis_index("sta") & len(send_refs)
    parts = [me ^ distance for distance in range(1, len(send_refs) + 1)]
    stack_parts(parts, rows_ref, used_ref, shift_ref, hankel_ref, inverse_ref, send_refs)


def keep_kernel(rows_ref, used_ref, shift_ref, hankel_ref, inverse_ref, keep_ref):
    me = lax.axis_index("sta") & (rows_ref.shape[2] - 1)
    stack_parts([me], rows_ref, used_ref, shift_ref, hankel_ref, inverse_ref, [keep_ref])


def flip(value, axis, mask):
    return lax.ppermute(value, axis, [(i, i ^ mask) for i in range(lax.axis_size(axis))])


def shards(waveform, fir_taps, templates, presence, moveout):
    block_rows, stations, templ_len = templates.shape
    owners, segments = lax.axis_size("sta"), lax.axis_size("tpl")
    sta = lax.axis_index("sta")
    samples = segments * waveform.shape[1]
    corr_len = samples - templ_len
    out_len = corr_len - SHIFT_MOST
    owned = block_rows // owners
    parts = min(owners, 4)
    part_rows = block_rows // parts
    vmem = pl.BlockSpec(memory_space=pltpu.VMEM)
    options = dict(
        compiler_params=pltpu.CompilerParams(vmem_limit_bytes=16 * 1024 * 1024),
        cost_estimate=pl.CostEstimate(flops=1 << 20, bytes_accessed=1 << 20, transcendentals=0),
    )
    rows = templates.transpose(1, 0, 2).reshape(stations, owners // parts, parts, owned, templ_len)
    own, toeplitz, used, shift = pl.pallas_call(
        functools.partial(columns_kernel, owners),
        out_shape=(
            jax.ShapeDtypeStruct(waveform.shape, jnp.float32),
            jax.ShapeDtypeStruct((PAIR, LANES), jnp.float32),
            jax.ShapeDtypeStruct((stations, parts, part_rows, LANES), jnp.float32),
            jax.ShapeDtypeStruct((stations, parts, part_rows, LANES), jnp.int32),
        ),
        in_specs=[vmem] * 4,
        out_specs=(vmem,) * 4,
        scratch_shapes=[pltpu.VMEM((8, LANES), jnp.float32)],
        name="columns",
        **options,
    )(waveform, fir_taps[None, :], presence.T, moveout.T)
    sent = {0: waveform}
    bit = segments // 2
    while bit >= 1:
        mask = bit | 1
        for d, piece in list(sent.items()):
            sent[d ^ mask] = flip(piece, "tpl", mask)
        if bit == segments // 2:
            sent[mask], rows = lax.optimization_barrier((sent[mask], rows))
        bit //= 2
    sent[0] = own
    *send, hankel, inverse = pl.pallas_call(
        functools.partial(send_kernel, segments),
        out_shape=(
            *[jax.ShapeDtypeStruct((owners // parts, owned, out_len), jnp.bfloat16)] * (parts - 1),
            jax.ShapeDtypeStruct((stations, LANES, samples), jnp.bfloat16),
            jax.ShapeDtypeStruct((stations, corr_len), jnp.float32),
        ),
        in_specs=[vmem] * (segments + 4),
        out_specs=(vmem,) * (parts + 1),
        scratch_shapes=[
            pltpu.VMEM((segments,) + waveform.shape, jnp.float32),
            pltpu.VMEM((samples // LANES * stations, LANES), jnp.float32),
            pltpu.VMEM((LANES, 3 * LANES), jnp.bfloat16),
            pltpu.VMEM((samples // LANES * stations, 3 * LANES), jnp.float32),
        ],
        name="send_parts",
        **options,
    )(*[sent[d] for d in range(segments)], toeplitz, rows, used, shift)
    stack = pl.pallas_call(
        keep_kernel,
        out_shape=jax.ShapeDtypeStruct((owners // parts, owned, out_len), jnp.float32),
        in_specs=[vmem] * 5,
        out_specs=vmem,
        name="keep_part",
        **options,
    )(rows, used, shift, hankel, inverse)
    for distance in range(1, parts):
        stack = stack + flip(send[distance - 1], "sta", distance).astype(jnp.float32)
    bit = parts
    while bit < owners:
        pairs = stack.reshape(stack.shape[0] // 2, 2, owned, out_len)
        side = (sta // bit) % 2
        stack = lax.dynamic_index_in_dim(pairs, side, 1, keepdims=False)
        other = lax.dynamic_index_in_dim(pairs, 1 - side, 1, keepdims=False).astype(jnp.bfloat16)
        stack = stack + flip(other, "sta", bit).astype(jnp.float32)
        bit *= 2
    return stack


def solution(mesh):
    placed = (P("sta", "tpl"), P(), P("tpl", "sta", None), P("tpl", "sta"), P("tpl", "sta"))
    return jax.shard_map(
        shards, mesh=mesh, in_specs=placed, out_specs=P("tpl", "sta", None), check_vma=False
    )
```

```python
import functools

import jax
import jax.numpy as jnp
from jax import lax
from jax.experimental import pallas as pl
from jax.experimental.pallas import tpu as pltpu
from jax.sharding import PartitionSpec as P

SHIFT_MOST = 128
LANES = 128
PAIR = 2 * LANES
epsilon = 1e-06


def lane_gather(values, index):
    return jnp.take_along_axis(values, index, axis=1, mode="promise_in_bounds")


def as_column(row):
    return jnp.broadcast_to(row, (LANES, row.shape[1])).T


def columns_kernel(owners, wave_in, taps_in, presence_ref, moveout_ref, wave_ref, toeplitz_ref, used_ref, shift_ref, row_ref):
    stations, parts, part_rows, _ = used_ref.shape
    owned = part_rows * parts // owners
    taps = taps_in.shape[1]
    wave_ref[...] = wave_in[...]
    row_ref[...] = jnp.zeros_like(row_ref)
    row_ref[0:1, 0:taps] = taps_in[...]
    sample = lax.broadcasted_iota(jnp.int32, (PAIR, LANES), 0)
    lane = lax.broadcasted_iota(jnp.int32, (PAIR, LANES), 1)
    tap = PAIR - 1 - lane - sample
    picked = lane_gather(jnp.broadcast_to(row_ref[0:1, :], (PAIR, LANES)), tap & (LANES - 1))
    toeplitz_ref[...] = jnp.where((tap >= 0) & (tap < taps), picked, 0.0)
    place = lax.broadcasted_iota(jnp.int32, (LANES, part_rows * parts), 1)
    part, rest = place // part_rows, place % part_rows
    old = (rest // owned * parts + part) * owned + rest % owned
    for s in range(stations):
        shift = lane_gather(jnp.broadcast_to(moveout_ref[s : s + 1, :], old.shape), old)
        shift_ref[s] = shift.T.reshape(shift_ref.shape[1:])
        used = lane_gather(jnp.broadcast_to(presence_ref[s : s + 1, :], old.shape), old)
        used_ref[s] = used.astype(jnp.float32).T.reshape(used_ref.shape[1:])


def stack_parts(parts, rows_ref, used_ref, shift_ref, hankel_ref, inverse_ref, out_refs):
    stations, groups, _, owned, templ_len = rows_ref.shape
    part_rows = groups * owned
    all_rows = len(parts) * part_rows
    corr_len = inverse_ref.shape[1]
    out_len = out_refs[0].shape[2]
    lag_pairs, time_pairs = templ_len // PAIR, corr_len // PAIR
    total = None
    for s in range(stations):
        rows = jnp.concatenate([rows_ref[s, :, p].reshape(part_rows, templ_len) for p in parts], axis=0)
        raw = [None] * time_pairs
        for offset in range(1, lag_pairs + time_pairs):
            uses = [(j, offset - lag_pairs + j) for j in range(lag_pairs) if 0 <= offset - lag_pairs + j < time_pairs]
            at = offset * PAIR
            window = jnp.concatenate(
                [hankel_ref[s, :, at : at + PAIR], hankel_ref[s, :, at - LANES : at - LANES + PAIR]], axis=0
            )
            left = jnp.concatenate([rows[:, j * PAIR : (j + 1) * PAIR] for j, _ in uses], axis=0)
            product = jnp.dot(left, window, preferred_element_type=jnp.float32)
            for k, (_, t) in enumerate(uses):
                part = product[k * all_rows : (k + 1) * all_rows]
                raw[t] = part if raw[t] is None else raw[t] + part
        correlation = jnp.concatenate(raw, axis=1) * inverse_ref[s : s + 1, :]
        wide = rows.astype(jnp.float32)
        norm = lax.rsqrt(jnp.sum(wide * wide, axis=1, keepdims=True) + epsilon)
        shift = jnp.concatenate([shift_ref[s, p] for p in parts], axis=0)
        lane = lax.broadcasted_iota(jnp.int32, shift.shape, 1)
        index = (PAIR - 1 - lane - shift) & (LANES - 1)
        later = lane + shift < LANES
        columns = [correlation[:, at : at + LANES] for at in range(0, corr_len, LANES)]
        last = corr_len // LANES - 1
        scale = norm * jnp.concatenate([used_ref[s, p] for p in parts], axis=0)
        aligned = [
            scale * lane_gather(jnp.where(later, columns[last - c], columns[last - 1 - c]), index)
            for c in range(out_len // LANES)
        ]
        total = aligned if total is None else [a + b for a, b in zip(total, aligned)]
    for k, out_ref in enumerate(out_refs):
        for c, part in enumerate(total):
            piece = part[k * part_rows : (k + 1) * part_rows].astype(out_ref.dtype)
            out_ref[:, :, c * LANES : (c + 1) * LANES] = piece.reshape(groups, owned, LANES)


def send_kernel(segments, *refs):
    segment_refs, (toeplitz_ref, rows_ref, used_ref, shift_ref, *send_refs) = refs[:segments], refs[segments:-6]
    hankel_ref, inverse_ref, wave_ref, series_ref, sums_of_ref, sums_ref = refs[-6:]
    stations, templ_len = rows_ref.shape[0], rows_ref.shape[-1]
    corr_len = inverse_ref.shape[1]
    seg_len = segment_refs[0].shape[1]
    blocks = len(segment_refs) * seg_len // LANES
    lags, times = templ_len // LANES, corr_len // LANES
    tpl = lax.axis_index("tpl")
    for distance, segment_ref in enumerate(segment_refs):
        wave_ref[tpl ^ distance] = segment_ref[...]
    places = [(c * LANES // seg_len, c * LANES % seg_len) for c in range(blocks)]
    block = jnp.concatenate([wave_ref[g, :, at : at + LANES] for g, at in places], axis=0)
    before = jnp.concatenate([jnp.zeros((stations, LANES), jnp.float32), block[:-stations]], axis=0)
    filtered = jnp.dot(
        jnp.concatenate([before, block], axis=1),
        toeplitz_ref[...],
        precision=lax.Precision.HIGHEST,
        preferred_element_type=jnp.float32,
    )
    series = filtered.astype(jnp.bfloat16).astype(jnp.float32)
    series_ref[...] = series
    row = lax.broadcasted_iota(jnp.int32, (LANES, LANES), 0)
    lane = lax.broadcasted_iota(jnp.int32, (LANES, LANES), 1)
    one = jnp.ones((LANES, LANES), jnp.float32)
    sums_of_ref[...] = jnp.concatenate(
        [jnp.where(row <= lane, one, 0.0), jnp.where(row > lane, one, 0.0), one], axis=1
    ).astype(jnp.bfloat16)
    squares = series * series
    high = squares.astype(jnp.bfloat16)
    low = (squares - high.astype(jnp.float32)).astype(jnp.bfloat16)
    sums_ref[...] = jnp.dot(high, sums_of_ref[...], preferred_element_type=jnp.float32) + jnp.dot(
        low, sums_of_ref[...], preferred_element_type=jnp.float32
    )

    def sums(c, kind):
        return sums_ref[c * stations : (c + 1) * stations, kind * LANES : (kind + 1) * LANES]

    for t in range(times):
        energy = sums(t, 0) + sums(t + lags, 1)
        for c in range(t + 1, t + lags):
            energy = energy + sums(c, 2)
        at = (times - 1 - t) * LANES
        inverse_ref[:, at : at + LANES] = lax.rsqrt(energy)
    for s in range(stations):
        whole = jnp.concatenate(
            [series_ref[c * stations + s : c * stations + s + 1, :] for c in reversed(range(blocks))], axis=1
        )
        ahead = pltpu.roll(
            jnp.broadcast_to(whole, (LANES, blocks * LANES)), 0, 1, stride=1, stride_axis=0
        )
        for c in range(1, blocks):
            hankel_ref[s, :, c * LANES : (c + 1) * LANES] = ahead[:, c * LANES : (c + 1) * LANES].astype(jnp.bfloat16)
    me = lax.axis_index("sta") & len(send_refs)
    parts = [me ^ distance for distance in range(1, len(send_refs) + 1)]
    stack_parts(parts, rows_ref, used_ref, shift_ref, hankel_ref, inverse_ref, send_refs)


def keep_kernel(rows_ref, used_ref, shift_ref, hankel_ref, inverse_ref, keep_ref):
    me = lax.axis_index("sta") & (rows_ref.shape[2] - 1)
    stack_parts([me], rows_ref, used_ref, shift_ref, hankel_ref, inverse_ref, [keep_ref])


def flip(value, sta_mask, tpl_mask):
    across = lax.axis_size("tpl")
    mask = sta_mask * across + tpl_mask
    pairs = [(i, i ^ mask) for i in range(lax.axis_size("sta") * across)]
    return lax.ppermute(value, ("sta", "tpl"), pairs)


def shards(waveform, fir_taps, templates, presence, moveout):
    block_rows, stations, templ_len = templates.shape
    owners, segments = lax.axis_size("sta"), lax.axis_size("tpl")
    sta = lax.axis_index("sta")
    samples = segments * waveform.shape[1]
    corr_len = samples - templ_len
    out_len = corr_len - SHIFT_MOST
    owned = block_rows // owners
    parts = min(owners, 4)
    part_rows = block_rows // parts
    vmem = pl.BlockSpec(memory_space=pltpu.VMEM)
    options = dict(
        compiler_params=pltpu.CompilerParams(vmem_limit_bytes=16 * 1024 * 1024),
        cost_estimate=pl.CostEstimate(flops=1 << 20, bytes_accessed=1 << 20, transcendentals=0),
    )
    rows = templates.transpose(1, 0, 2).reshape(stations, owners // parts, parts, owned, templ_len)
    own, toeplitz, used, shift = pl.pallas_call(
        functools.partial(columns_kernel, owners),
        out_shape=(
            jax.ShapeDtypeStruct(waveform.shape, jnp.float32),
            jax.ShapeDtypeStruct((PAIR, LANES), jnp.float32),
            jax.ShapeDtypeStruct((stations, parts, part_rows, LANES), jnp.float32),
            jax.ShapeDtypeStruct((stations, parts, part_rows, LANES), jnp.int32),
        ),
        in_specs=[vmem] * 4,
        out_specs=(vmem,) * 4,
        scratch_shapes=[pltpu.VMEM((8, LANES), jnp.float32)],
        name="columns",
        **options,
    )(waveform, fir_taps[None, :], presence.T, moveout.T)
    sent = {0: waveform}
    bit = segments // 2
    while bit >= 1:
        mask = bit | 1
        for d, piece in list(sent.items()):
            sent[d ^ mask] = flip(piece, 0, mask)
        if bit == segments // 2:
            sent[mask], rows = lax.optimization_barrier((sent[mask], rows))
        bit //= 2
    sent[0] = own
    *send, hankel, inverse = pl.pallas_call(
        functools.partial(send_kernel, segments),
        out_shape=(
            *[jax.ShapeDtypeStruct((owners // parts, owned, out_len), jnp.bfloat16)] * (parts - 1),
            jax.ShapeDtypeStruct((stations, LANES, samples), jnp.bfloat16),
            jax.ShapeDtypeStruct((stations, corr_len), jnp.float32),
        ),
        in_specs=[vmem] * (segments + 4),
        out_specs=(vmem,) * (parts + 1),
        scratch_shapes=[
            pltpu.VMEM((segments,) + waveform.shape, jnp.float32),
            pltpu.VMEM((samples // LANES * stations, LANES), jnp.float32),
            pltpu.VMEM((LANES, 3 * LANES), jnp.bfloat16),
            pltpu.VMEM((samples // LANES * stations, 3 * LANES), jnp.float32),
        ],
        name="send_parts",
        **options,
    )(*[sent[d] for d in range(segments)], toeplitz, rows, used, shift)
    stack = pl.pallas_call(
        keep_kernel,
        out_shape=jax.ShapeDtypeStruct((owners // parts, owned, out_len), jnp.float32),
        in_specs=[vmem] * 5,
        out_specs=vmem,
        name="keep_part",
        **options,
    )(rows, used, shift, hankel, inverse)
    rounds = [parts]
    while rounds[-1] < owners:
        rounds.append(rounds[-1] * 2)
    turns = len(rounds) // 2 * 2 if segments > 1 else 0
    for number, reach in enumerate(rounds):
        turn = 1 if number < turns else 0
        if number == 0:
            moved = [(distance, send[distance - 1]) for distance in range(1, parts)]
        else:
            bit = reach // 2
            pairs = stack.reshape(stack.shape[0] // 2, 2, owned, out_len)
            side = (sta // bit) % 2
            stack = lax.dynamic_index_in_dim(pairs, side, 1, keepdims=False)
            moved = [(bit, lax.dynamic_index_in_dim(pairs, 1 - side, 1, keepdims=False).astype(jnp.bfloat16))]
        arrived = [flip(piece, distance, turn) for distance, piece in moved]
        if turn:
            if number == 0:
                stack, _ = lax.optimization_barrier((stack, arrived[-1]))
            pieces = [stack[:, :, at : at + LANES] for at in range(0, out_len, LANES)]
            stack = jnp.concatenate([flip(piece, 0, turn) for piece in pieces], axis=2)
        for piece in arrived:
            stack = stack + piece.astype(jnp.float32)
    return stack


def solution(mesh):
    placed = (P("sta", "tpl"), P(), P("tpl", "sta", None), P("tpl", "sta"), P("tpl", "sta"))
    return jax.shard_map(
        shards, mesh=mesh, in_specs=placed, out_specs=P("tpl", "sta", None), check_vma=False
    )
```

```python
import functools

import jax
import jax.numpy as jnp
from jax import lax
from jax.experimental import pallas as pl
from jax.experimental.pallas import tpu as pltpu
from jax.sharding import PartitionSpec as P

SHIFT_MOST = 128
LANES = 128
PAIR = 2 * LANES
epsilon = 1e-06


def lane_gather(values, index):
    return jnp.take_along_axis(values, index, axis=1, mode="promise_in_bounds")


def as_column(row):
    return jnp.broadcast_to(row, (LANES, row.shape[1])).T


def columns_kernel(owners, wave_in, taps_in, presence_ref, moveout_ref, wave_ref, toeplitz_ref, used_ref, shift_ref, row_ref):
    stations, parts, part_rows, _ = used_ref.shape
    owned = part_rows * parts // owners
    taps = taps_in.shape[1]
    wave_ref[...] = wave_in[...]
    row_ref[...] = jnp.zeros_like(row_ref)
    row_ref[0:1, 0:taps] = taps_in[...]
    sample = lax.broadcasted_iota(jnp.int32, (PAIR, LANES), 0)
    lane = lax.broadcasted_iota(jnp.int32, (PAIR, LANES), 1)
    tap = PAIR - 1 - lane - sample
    picked = lane_gather(jnp.broadcast_to(row_ref[0:1, :], (PAIR, LANES)), tap & (LANES - 1))
    toeplitz_ref[...] = jnp.where((tap >= 0) & (tap < taps), picked, 0.0)
    place = lax.broadcasted_iota(jnp.int32, (LANES, part_rows * parts), 1)
    part, rest = place // part_rows, place % part_rows
    old = (rest // owned * parts + part) * owned + rest % owned
    for s in range(stations):
        shift = lane_gather(jnp.broadcast_to(moveout_ref[s : s + 1, :], old.shape), old)
        shift_ref[s] = shift.T.reshape(shift_ref.shape[1:])
        used = lane_gather(jnp.broadcast_to(presence_ref[s : s + 1, :], old.shape), old)
        used_ref[s] = used.astype(jnp.float32).T.reshape(used_ref.shape[1:])


def stack_parts(parts, rows_ref, used_ref, shift_ref, hankel_ref, inverse_ref, out_refs):
    stations, groups, _, owned, templ_len = rows_ref.shape
    part_rows = groups * owned
    all_rows = len(parts) * part_rows
    corr_len = inverse_ref.shape[1]
    out_len = out_refs[0].shape[2]
    lag_pairs, time_pairs = templ_len // PAIR, corr_len // PAIR
    total = None
    for s in range(stations):
        rows = jnp.concatenate([rows_ref[s, :, p].reshape(part_rows, templ_len) for p in parts], axis=0)
        raw = [None] * time_pairs
        for offset in range(1, lag_pairs + time_pairs):
            uses = [(j, offset - lag_pairs + j) for j in range(lag_pairs) if 0 <= offset - lag_pairs + j < time_pairs]
            at = offset * PAIR
            window = jnp.concatenate(
                [hankel_ref[s, :, at : at + PAIR], hankel_ref[s, :, at - LANES : at - LANES + PAIR]], axis=0
            )
            left = jnp.concatenate([rows[:, j * PAIR : (j + 1) * PAIR] for j, _ in uses], axis=0)
            product = jnp.dot(left, window, preferred_element_type=jnp.float32)
            for k, (_, t) in enumerate(uses):
                part = product[k * all_rows : (k + 1) * all_rows]
                raw[t] = part if raw[t] is None else raw[t] + part
        correlation = jnp.concatenate(raw, axis=1) * inverse_ref[s : s + 1, :]
        wide = rows.astype(jnp.float32)
        norm = lax.rsqrt(jnp.sum(wide * wide, axis=1, keepdims=True) + epsilon)
        shift = jnp.concatenate([shift_ref[s, p] for p in parts], axis=0)
        lane = lax.broadcasted_iota(jnp.int32, shift.shape, 1)
        index = (PAIR - 1 - lane - shift) & (LANES - 1)
        later = lane + shift < LANES
        columns = [correlation[:, at : at + LANES] for at in range(0, corr_len, LANES)]
        last = corr_len // LANES - 1
        scale = norm * jnp.concatenate([used_ref[s, p] for p in parts], axis=0)
        aligned = [
            scale * lane_gather(jnp.where(later, columns[last - c], columns[last - 1 - c]), index)
            for c in range(out_len // LANES)
        ]
        total = aligned if total is None else [a + b for a, b in zip(total, aligned)]
    for k, out_ref in enumerate(out_refs):
        for c, part in enumerate(total):
            piece = part[k * part_rows : (k + 1) * part_rows].astype(out_ref.dtype)
            out_ref[:, :, c * LANES : (c + 1) * LANES] = piece.reshape(groups, owned, LANES)


def send_kernel(segments, *refs):
    segment_refs, (toeplitz_ref, rows_ref, used_ref, shift_ref, *send_refs) = refs[:segments], refs[segments:-6]
    hankel_ref, inverse_ref, wave_ref, series_ref, sums_of_ref, sums_ref = refs[-6:]
    stations, templ_len = rows_ref.shape[0], rows_ref.shape[-1]
    corr_len = inverse_ref.shape[1]
    seg_len = segment_refs[0].shape[1]
    blocks = len(segment_refs) * seg_len // LANES
    lags, times = templ_len // LANES, corr_len // LANES
    tpl = lax.axis_index("tpl")
    for distance, segment_ref in enumerate(segment_refs):
        wave_ref[tpl ^ distance] = segment_ref[...]
    places = [(c * LANES // seg_len, c * LANES % seg_len) for c in range(blocks)]
    block = jnp.concatenate([wave_ref[g, :, at : at + LANES] for g, at in places], axis=0)
    before = jnp.concatenate([jnp.zeros((stations, LANES), jnp.float32), block[:-stations]], axis=0)
    filtered = jnp.dot(
        jnp.concatenate([before, block], axis=1),
        toeplitz_ref[...],
        precision=lax.Precision.HIGHEST,
        preferred_element_type=jnp.float32,
    )
    series = filtered.astype(jnp.bfloat16).astype(jnp.float32)
    series_ref[...] = series
    row = lax.broadcasted_iota(jnp.int32, (LANES, LANES), 0)
    lane = lax.broadcasted_iota(jnp.int32, (LANES, LANES), 1)
    one = jnp.ones((LANES, LANES), jnp.float32)
    sums_of_ref[...] = jnp.concatenate(
        [jnp.where(row <= lane, one, 0.0), jnp.where(row > lane, one, 0.0), one], axis=1
    ).astype(jnp.bfloat16)
    squares = series * series
    high = squares.astype(jnp.bfloat16)
    low = (squares - high.astype(jnp.float32)).astype(jnp.bfloat16)
    sums_ref[...] = jnp.dot(high, sums_of_ref[...], preferred_element_type=jnp.float32) + jnp.dot(
        low, sums_of_ref[...], preferred_element_type=jnp.float32
    )

    def sums(c, kind):
        return sums_ref[c * stations : (c + 1) * stations, kind * LANES : (kind + 1) * LANES]

    for t in range(times):
        energy = sums(t, 0) + sums(t + lags, 1)
        for c in range(t + 1, t + lags):
            energy = energy + sums(c, 2)
        at = (times - 1 - t) * LANES
        inverse_ref[:, at : at + LANES] = lax.rsqrt(energy)
    for s in range(stations):
        whole = jnp.concatenate(
            [series_ref[c * stations + s : c * stations + s + 1, :] for c in reversed(range(blocks))], axis=1
        )
        ahead = pltpu.roll(
            jnp.broadcast_to(whole, (LANES, blocks * LANES)), 0, 1, stride=1, stride_axis=0
        )
        for c in range(1, blocks):
            hankel_ref[s, :, c * LANES : (c + 1) * LANES] = ahead[:, c * LANES : (c + 1) * LANES].astype(jnp.bfloat16)
    me = lax.axis_index("sta") & len(send_refs)
    parts = [me ^ distance for distance in range(1, len(send_refs) + 1)]
    stack_parts(parts, rows_ref, used_ref, shift_ref, hankel_ref, inverse_ref, send_refs)


def keep_kernel(rows_ref, used_ref, shift_ref, hankel_ref, inverse_ref, keep_ref):
    me = lax.axis_index("sta") & (rows_ref.shape[2] - 1)
    stack_parts([me], rows_ref, used_ref, shift_ref, hankel_ref, inverse_ref, [keep_ref])


def flip(value, sta_mask, tpl_mask):
    across = lax.axis_size("tpl")
    mask = sta_mask * across + tpl_mask
    pairs = [(i, i ^ mask) for i in range(lax.axis_size("sta") * across)]
    return lax.ppermute(value, ("sta", "tpl"), pairs)


def shards(waveform, fir_taps, templates, presence, moveout):
    block_rows, stations, templ_len = templates.shape
    owners, segments = lax.axis_size("sta"), lax.axis_size("tpl")
    sta = lax.axis_index("sta")
    samples = segments * waveform.shape[1]
    corr_len = samples - templ_len
    out_len = corr_len - SHIFT_MOST
    owned = block_rows // owners
    parts = min(owners, 4)
    part_rows = block_rows // parts
    vmem = pl.BlockSpec(memory_space=pltpu.VMEM)
    options = dict(
        compiler_params=pltpu.CompilerParams(vmem_limit_bytes=16 * 1024 * 1024),
        cost_estimate=pl.CostEstimate(flops=1 << 20, bytes_accessed=1 << 20, transcendentals=0),
    )
    rows = templates.transpose(1, 0, 2).reshape(stations, owners // parts, parts, owned, templ_len)
    own, toeplitz, used, shift = pl.pallas_call(
        functools.partial(columns_kernel, owners),
        out_shape=(
            jax.ShapeDtypeStruct(waveform.shape, jnp.float32),
            jax.ShapeDtypeStruct((PAIR, LANES), jnp.float32),
            jax.ShapeDtypeStruct((stations, parts, part_rows, LANES), jnp.float32),
            jax.ShapeDtypeStruct((stations, parts, part_rows, LANES), jnp.int32),
        ),
        in_specs=[vmem] * 4,
        out_specs=(vmem,) * 4,
        scratch_shapes=[pltpu.VMEM((8, LANES), jnp.float32)],
        name="columns",
        **options,
    )(waveform, fir_taps[None, :], presence.T, moveout.T)
    sent = {0: waveform}
    bit = segments // 2
    while bit >= 1:
        mask = bit | 1
        for d, piece in list(sent.items()):
            sent[d ^ mask] = flip(piece, 0, mask)
        if bit == segments // 2:
            sent[mask], rows = lax.optimization_barrier((sent[mask], rows))
        bit //= 2
    sent[0] = own
    *send, hankel, inverse = pl.pallas_call(
        functools.partial(send_kernel, segments),
        out_shape=(
            *[jax.ShapeDtypeStruct((owners // parts, owned, out_len), jnp.bfloat16)] * (parts - 1),
            jax.ShapeDtypeStruct((stations, LANES, samples), jnp.bfloat16),
            jax.ShapeDtypeStruct((stations, corr_len), jnp.float32),
        ),
        in_specs=[vmem] * (segments + 4),
        out_specs=(vmem,) * (parts + 1),
        scratch_shapes=[
            pltpu.VMEM((segments,) + waveform.shape, jnp.float32),
            pltpu.VMEM((samples // LANES * stations, LANES), jnp.float32),
            pltpu.VMEM((LANES, 3 * LANES), jnp.bfloat16),
            pltpu.VMEM((samples // LANES * stations, 3 * LANES), jnp.float32),
        ],
        name="send_parts",
        **options,
    )(*[sent[d] for d in range(segments)], toeplitz, rows, used, shift)
    stack = pl.pallas_call(
        keep_kernel,
        out_shape=jax.ShapeDtypeStruct((owners // parts, owned, out_len), jnp.float32),
        in_specs=[vmem] * 5,
        out_specs=vmem,
        name="keep_part",
        **options,
    )(rows, used, shift, hankel, inverse)
    rounds = [parts]
    while rounds[-1] < owners:
        rounds.append(rounds[-1] * 2)
    turns = len(rounds) // 2 * 2 if segments > 1 else 0
    for number, reach in enumerate(rounds):
        turn = 1 if number < turns else 0
        if number == 0:
            moved = [(distance, send[distance - 1]) for distance in range(1, parts)]
        else:
            bit = reach // 2
            pairs = stack.reshape(stack.shape[0] // 2, 2, owned, out_len)
            side = (sta // bit) % 2
            stack = lax.dynamic_index_in_dim(pairs, side, 1, keepdims=False)
            moved = [(bit, lax.dynamic_index_in_dim(pairs, 1 - side, 1, keepdims=False))]
        arrived = [flip(piece, distance, turn) for distance, piece in moved]
        if turn:
            if number == 0:
                stack, _ = lax.optimization_barrier((stack, arrived[-1]))
            if number == 0:
                pieces = [stack[:, :, at : at + LANES] for at in range(0, out_len, LANES)]
                stack = jnp.concatenate([flip(piece, 0, turn) for piece in pieces], axis=2)
            else:
                pieces = [stack[:, : owned // 2], stack[:, owned // 2 :]]
                stack = jnp.concatenate([flip(piece, 0, turn) for piece in pieces], axis=1)
        for piece in arrived:
            stack = stack + piece.astype(jnp.float32)
    return stack


def solution(mesh):
    placed = (P("sta", "tpl"), P(), P("tpl", "sta", None), P("tpl", "sta"), P("tpl", "sta"))
    return jax.shard_map(
        shards, mesh=mesh, in_specs=placed, out_specs=P("tpl", "sta", None), check_vma=False
    )
```

```python
import functools

import jax
import jax.numpy as jnp
from jax import lax
from jax.experimental import pallas as pl
from jax.experimental.pallas import tpu as pltpu
from jax.sharding import PartitionSpec as P

SHIFT_MOST = 128
LANES = 128
PAIR = 2 * LANES
epsilon = 1e-06


def lane_gather(values, index):
    return jnp.take_along_axis(values, index, axis=1, mode="promise_in_bounds")


def as_column(row):
    return jnp.broadcast_to(row, (LANES, row.shape[1])).T


def columns_kernel(owners, wave_in, taps_in, presence_ref, moveout_ref, wave_ref, toeplitz_ref, used_ref, shift_ref, row_ref):
    stations, parts, part_rows, _ = used_ref.shape
    owned = part_rows * parts // owners
    taps = taps_in.shape[1]
    wave_ref[...] = wave_in[...]
    row_ref[...] = jnp.zeros_like(row_ref)
    row_ref[0:1, 0:taps] = taps_in[...]
    sample = lax.broadcasted_iota(jnp.int32, (PAIR, LANES), 0)
    lane = lax.broadcasted_iota(jnp.int32, (PAIR, LANES), 1)
    tap = PAIR - 1 - lane - sample
    picked = lane_gather(jnp.broadcast_to(row_ref[0:1, :], (PAIR, LANES)), tap & (LANES - 1))
    toeplitz_ref[...] = jnp.where((tap >= 0) & (tap < taps), picked, 0.0)
    place = lax.broadcasted_iota(jnp.int32, (LANES, part_rows * parts), 1)
    part, rest = place // part_rows, place % part_rows
    old = (rest // owned * parts + part) * owned + rest % owned
    for s in range(stations):
        shift = lane_gather(jnp.broadcast_to(moveout_ref[s : s + 1, :], old.shape), old)
        shift_ref[s] = shift.T.reshape(shift_ref.shape[1:])
        used = lane_gather(jnp.broadcast_to(presence_ref[s : s + 1, :], old.shape), old)
        used_ref[s] = used.astype(jnp.float32).T.reshape(used_ref.shape[1:])


def stack_parts(parts, rows_ref, used_ref, shift_ref, hankel_ref, inverse_ref, out_refs):
    stations, groups, _, owned, templ_len = rows_ref.shape
    part_rows = groups * owned
    all_rows = len(parts) * part_rows
    corr_len = inverse_ref.shape[1]
    out_len = out_refs[0].shape[2]
    lag_pairs, time_pairs = templ_len // PAIR, corr_len // PAIR
    total = None
    for s in range(stations):
        rows = jnp.concatenate([rows_ref[s, :, p].reshape(part_rows, templ_len) for p in parts], axis=0)
        raw = [None] * time_pairs
        for offset in reversed(range(1, lag_pairs + time_pairs)):
            uses = [(j, offset - lag_pairs + j) for j in range(lag_pairs) if 0 <= offset - lag_pairs + j < time_pairs]
            at = offset * PAIR
            window = jnp.concatenate(
                [hankel_ref[s, :, at : at + PAIR], hankel_ref[s, :, at - LANES : at - LANES + PAIR]], axis=0
            )
            left = jnp.concatenate([rows[:, j * PAIR : (j + 1) * PAIR] for j, _ in uses], axis=0)
            product = jnp.dot(left, window, preferred_element_type=jnp.float32)
            for k, (_, t) in enumerate(uses):
                part = product[k * all_rows : (k + 1) * all_rows]
                raw[t] = part if raw[t] is None else raw[t] + part
        correlation = jnp.concatenate(raw, axis=1) * inverse_ref[s : s + 1, :]
        wide = rows.astype(jnp.float32)
        norm = lax.rsqrt(jnp.sum(wide * wide, axis=1, keepdims=True) + epsilon)
        shift = jnp.concatenate([shift_ref[s, p] for p in parts], axis=0)
        lane = lax.broadcasted_iota(jnp.int32, shift.shape, 1)
        index = (PAIR - 1 - lane - shift) & (LANES - 1)
        later = lane + shift < LANES
        columns = [correlation[:, at : at + LANES] for at in range(0, corr_len, LANES)]
        last = corr_len // LANES - 1
        scale = norm * jnp.concatenate([used_ref[s, p] for p in parts], axis=0)
        aligned = [
            scale * lane_gather(jnp.where(later, columns[last - c], columns[last - 1 - c]), index)
            for c in range(out_len // LANES)
        ]
        total = aligned if total is None else [a + b for a, b in zip(total, aligned)]
    for k, out_ref in enumerate(out_refs):
        for c, part in enumerate(total):
            piece = part[k * part_rows : (k + 1) * part_rows].astype(out_ref.dtype)
            out_ref[:, :, c * LANES : (c + 1) * LANES] = piece.reshape(groups, owned, LANES)


def send_kernel(segments, *refs):
    segment_refs, (toeplitz_ref, rows_ref, used_ref, shift_ref, *send_refs) = refs[:segments], refs[segments:-6]
    hankel_ref, inverse_ref, wave_ref, series_ref, sums_of_ref, sums_ref = refs[-6:]
    stations, templ_len = rows_ref.shape[0], rows_ref.shape[-1]
    corr_len = inverse_ref.shape[1]
    seg_len = segment_refs[0].shape[1]
    blocks = len(segment_refs) * seg_len // LANES
    lags, times = templ_len // LANES, corr_len // LANES
    tpl = lax.axis_index("tpl")
    for distance, segment_ref in enumerate(segment_refs):
        wave_ref[tpl ^ distance] = segment_ref[...]
    places = [(c * LANES // seg_len, c * LANES % seg_len) for c in range(blocks)]
    block = jnp.concatenate([wave_ref[g, :, at : at + LANES] for g, at in places], axis=0)
    before = jnp.concatenate([jnp.zeros((stations, LANES), jnp.float32), block[:-stations]], axis=0)
    filtered = jnp.dot(
        jnp.concatenate([before, block], axis=1),
        toeplitz_ref[...],
        precision=lax.Precision.HIGHEST,
        preferred_element_type=jnp.float32,
    )
    series = filtered.astype(jnp.bfloat16).astype(jnp.float32)
    series_ref[...] = series
    row = lax.broadcasted_iota(jnp.int32, (LANES, LANES), 0)
    lane = lax.broadcasted_iota(jnp.int32, (LANES, LANES), 1)
    one = jnp.ones((LANES, LANES), jnp.float32)
    sums_of_ref[...] = jnp.concatenate(
        [jnp.where(row <= lane, one, 0.0), jnp.where(row > lane, one, 0.0), one], axis=1
    ).astype(jnp.bfloat16)
    squares = series * series
    high = squares.astype(jnp.bfloat16)
    low = (squares - high.astype(jnp.float32)).astype(jnp.bfloat16)
    sums_ref[...] = jnp.dot(high, sums_of_ref[...], preferred_element_type=jnp.float32) + jnp.dot(
        low, sums_of_ref[...], preferred_element_type=jnp.float32
    )

    def sums(c, kind):
        return sums_ref[c * stations : (c + 1) * stations, kind * LANES : (kind + 1) * LANES]

    for t in range(times):
        energy = sums(t, 0) + sums(t + lags, 1)
        for c in range(t + 1, t + lags):
            energy = energy + sums(c, 2)
        at = (times - 1 - t) * LANES
        inverse_ref[:, at : at + LANES] = lax.rsqrt(energy)
    for s in range(stations):
        whole = jnp.concatenate(
            [series_ref[c * stations + s : c * stations + s + 1, :] for c in reversed(range(blocks))], axis=1
        )
        ahead = pltpu.roll(
            jnp.broadcast_to(whole, (LANES, blocks * LANES)), 0, 1, stride=1, stride_axis=0
        )
        for c in range(1, blocks):
            hankel_ref[s, :, c * LANES : (c + 1) * LANES] = ahead[:, c * LANES : (c + 1) * LANES].astype(jnp.bfloat16)
    me = lax.axis_index("sta") & len(send_refs)
    parts = [me ^ distance for distance in range(1, len(send_refs) + 1)]
    stack_parts(parts, rows_ref, used_ref, shift_ref, hankel_ref, inverse_ref, send_refs)


def keep_kernel(rows_ref, used_ref, shift_ref, hankel_ref, inverse_ref, keep_ref):
    me = lax.axis_index("sta") & (rows_ref.shape[2] - 1)
    stack_parts([me], rows_ref, used_ref, shift_ref, hankel_ref, inverse_ref, [keep_ref])


def flip(value, sta_mask, tpl_mask):
    across = lax.axis_size("tpl")
    mask = sta_mask * across + tpl_mask
    pairs = [(i, i ^ mask) for i in range(lax.axis_size("sta") * across)]
    return lax.ppermute(value, ("sta", "tpl"), pairs)


def shards(waveform, fir_taps, templates, presence, moveout):
    block_rows, stations, templ_len = templates.shape
    owners, segments = lax.axis_size("sta"), lax.axis_size("tpl")
    sta = lax.axis_index("sta")
    samples = segments * waveform.shape[1]
    corr_len = samples - templ_len
    out_len = corr_len - SHIFT_MOST
    owned = block_rows // owners
    parts = min(owners, 4)
    part_rows = block_rows // parts
    vmem = pl.BlockSpec(memory_space=pltpu.VMEM)
    options = dict(
        compiler_params=pltpu.CompilerParams(vmem_limit_bytes=16 * 1024 * 1024),
        cost_estimate=pl.CostEstimate(flops=1 << 20, bytes_accessed=1 << 20, transcendentals=0),
    )
    rows = templates.transpose(1, 0, 2).reshape(stations, owners // parts, parts, owned, templ_len)
    own, toeplitz, used, shift = pl.pallas_call(
        functools.partial(columns_kernel, owners),
        out_shape=(
            jax.ShapeDtypeStruct(waveform.shape, jnp.float32),
            jax.ShapeDtypeStruct((PAIR, LANES), jnp.float32),
            jax.ShapeDtypeStruct((stations, parts, part_rows, LANES), jnp.float32),
            jax.ShapeDtypeStruct((stations, parts, part_rows, LANES), jnp.int32),
        ),
        in_specs=[vmem] * 4,
        out_specs=(vmem,) * 4,
        scratch_shapes=[pltpu.VMEM((8, LANES), jnp.float32)],
        name="columns",
        **options,
    )(waveform, fir_taps[None, :], presence.T, moveout.T)
    sent = {0: waveform}
    bit = segments // 2
    while bit >= 1:
        mask = bit | 1
        for d, piece in list(sent.items()):
            sent[d ^ mask] = flip(piece, 0, mask)
        if bit == segments // 2:
            sent[mask], rows = lax.optimization_barrier((sent[mask], rows))
        bit //= 2
    sent[0] = own
    *send, hankel, inverse = pl.pallas_call(
        functools.partial(send_kernel, segments),
        out_shape=(
            *[jax.ShapeDtypeStruct((owners // parts, owned, out_len), jnp.bfloat16)] * (parts - 1),
            jax.ShapeDtypeStruct((stations, LANES, samples), jnp.bfloat16),
            jax.ShapeDtypeStruct((stations, corr_len), jnp.float32),
        ),
        in_specs=[vmem] * (segments + 4),
        out_specs=(vmem,) * (parts + 1),
        scratch_shapes=[
            pltpu.VMEM((segments,) + waveform.shape, jnp.float32),
            pltpu.VMEM((samples // LANES * stations, LANES), jnp.float32),
            pltpu.VMEM((LANES, 3 * LANES), jnp.bfloat16),
            pltpu.VMEM((samples // LANES * stations, 3 * LANES), jnp.float32),
        ],
        name="send_parts",
        **options,
    )(*[sent[d] for d in range(segments)], toeplitz, rows, used, shift)
    stack = pl.pallas_call(
        keep_kernel,
        out_shape=jax.ShapeDtypeStruct((owners // parts, owned, out_len), jnp.float32),
        in_specs=[vmem] * 5,
        out_specs=vmem,
        name="keep_part",
        **options,
    )(rows, used, shift, hankel, inverse)
    rounds = [parts]
    while rounds[-1] < owners:
        rounds.append(rounds[-1] * 2)
    turns = len(rounds) // 2 * 2 if segments > 1 else 0
    for number, reach in enumerate(rounds):
        turn = 1 if number < turns else 0
        if number == 0:
            moved = [(distance, send[distance - 1]) for distance in range(1, parts)]
        else:
            bit = reach // 2
            pairs = stack.reshape(stack.shape[0] // 2, 2, owned, out_len)
            side = (sta // bit) % 2
            stack = lax.dynamic_index_in_dim(pairs, side, 1, keepdims=False)
            moved = [(bit, lax.dynamic_index_in_dim(pairs, 1 - side, 1, keepdims=False))]
        arrived = [flip(piece, distance, turn) for distance, piece in moved]
        if turn:
            if number == 0:
                stack, _ = lax.optimization_barrier((stack, arrived[-1]))
            if number == 0:
                pieces = [stack[:, :, at : at + LANES] for at in range(0, out_len, LANES)]
                stack = jnp.concatenate([flip(piece, 0, turn) for piece in pieces], axis=2)
            else:
                pieces = [stack[:, : owned // 2], stack[:, owned // 2 :]]
                stack = jnp.concatenate([flip(piece, 0, turn) for piece in pieces], axis=1)
        for piece in arrived:
            stack = stack + piece.astype(jnp.float32)
    return stack


def solution(mesh):
    placed = (P("sta", "tpl"), P(), P("tpl", "sta", None), P("tpl", "sta"), P("tpl", "sta"))
    return jax.shard_map(
        shards, mesh=mesh, in_specs=placed, out_specs=P("tpl", "sta", None), check_vma=False
    )
```

```python
import functools

import jax
import jax.numpy as jnp
from jax import lax
from jax.experimental import pallas as pl
from jax.experimental.pallas import tpu as pltpu
from jax.sharding import PartitionSpec as P

SHIFT_MOST = 128
LANES = 128
PAIR = 2 * LANES
epsilon = 1e-06


def lane_gather(values, index):
    return jnp.take_along_axis(values, index, axis=1, mode="promise_in_bounds")


def as_column(row):
    return jnp.broadcast_to(row, (LANES, row.shape[1])).T


def columns_kernel(owners, wave_in, taps_in, presence_ref, moveout_ref, wave_ref, toeplitz_ref, used_ref, shift_ref, row_ref):
    stations, parts, part_rows, _ = used_ref.shape
    owned = part_rows * parts // owners
    taps = taps_in.shape[1]
    wave_ref[...] = wave_in[...]
    row_ref[...] = jnp.zeros_like(row_ref)
    row_ref[0:1, 0:taps] = taps_in[...]
    sample = lax.broadcasted_iota(jnp.int32, (PAIR, LANES), 0)
    lane = lax.broadcasted_iota(jnp.int32, (PAIR, LANES), 1)
    tap = PAIR - 1 - lane - sample
    picked = lane_gather(jnp.broadcast_to(row_ref[0:1, :], (PAIR, LANES)), tap & (LANES - 1))
    toeplitz_ref[...] = jnp.where((tap >= 0) & (tap < taps), picked, 0.0)
    place = lax.broadcasted_iota(jnp.int32, (LANES, part_rows * parts), 1)
    part, rest = place // part_rows, place % part_rows
    old = (rest // owned * parts + part) * owned + rest % owned
    for s in range(stations):
        shift = lane_gather(jnp.broadcast_to(moveout_ref[s : s + 1, :], old.shape), old)
        shift_ref[s] = shift.T.reshape(shift_ref.shape[1:])
        used = lane_gather(jnp.broadcast_to(presence_ref[s : s + 1, :], old.shape), old)
        used_ref[s] = used.astype(jnp.float32).T.reshape(used_ref.shape[1:])


def stack_parts(parts, rows_ref, used_ref, shift_ref, hankel_ref, inverse_ref, out_refs):
    stations, groups, _, owned, templ_len = rows_ref.shape
    part_rows = groups * owned
    corr_len = inverse_ref.shape[1]
    out_len = out_refs[0].shape[2]
    lag_pairs, time_pairs = templ_len // PAIR, corr_len // PAIR
    total = None
    for s in range(stations):
        rows = jnp.concatenate([rows_ref[s, :, p].reshape(part_rows, templ_len) for p in parts], axis=0)
        raw = [None] * time_pairs
        for offset in reversed(range(1, lag_pairs + time_pairs)):
            uses = [(j, offset - lag_pairs + j) for j in range(lag_pairs) if 0 <= offset - lag_pairs + j < time_pairs]
            at = offset * PAIR
            window = jnp.concatenate(
                [hankel_ref[s, :, at : at + PAIR], hankel_ref[s, :, at - LANES : at - LANES + PAIR]], axis=0
            )
            for j, t in uses:
                part = jnp.dot(rows[:, j * PAIR : (j + 1) * PAIR], window, preferred_element_type=jnp.float32)
                raw[t] = part if raw[t] is None else raw[t] + part
        inverse = inverse_ref[s : s + 1, :]
        last = corr_len // LANES - 1
        done = []
        for number, p in enumerate(parts):
            first, end = number * part_rows, (number + 1) * part_rows
            wide = rows[first:end].astype(jnp.float32)
            scale = lax.rsqrt(jnp.sum(wide * wide, axis=1, keepdims=True) + epsilon) * used_ref[s, p]
            shift = shift_ref[s, p]
            lane = lax.broadcasted_iota(jnp.int32, shift.shape, 1)
            index = (PAIR - 1 - lane - shift) & (LANES - 1)
            later = lane + shift < LANES
            columns = [
                values[first:end, at : at + LANES] * inverse[:, t * PAIR + at : t * PAIR + at + LANES]
                for t, values in enumerate(raw)
                for at in range(0, PAIR, LANES)
            ]
            done.append(
                [
                    lane_gather(scale * jnp.where(later, columns[last - c], columns[last - 1 - c]), index)
                    for c in range(out_len // LANES)
                ]
            )
        aligned = [jnp.concatenate([part[c] for part in done], axis=0) for c in range(out_len // LANES)]
        total = aligned if total is None else [a + b for a, b in zip(total, aligned)]
    for k, out_ref in enumerate(out_refs):
        for c, part in enumerate(total):
            piece = part[k * part_rows : (k + 1) * part_rows].astype(out_ref.dtype)
            out_ref[:, :, c * LANES : (c + 1) * LANES] = piece.reshape(groups, owned, LANES)


def send_kernel(segments, *refs):
    segment_refs, (toeplitz_ref, rows_ref, used_ref, shift_ref, *send_refs) = refs[:segments], refs[segments:-6]
    hankel_ref, inverse_ref, wave_ref, series_ref, sums_of_ref, sums_ref = refs[-6:]
    stations, templ_len = rows_ref.shape[0], rows_ref.shape[-1]
    corr_len = inverse_ref.shape[1]
    seg_len = segment_refs[0].shape[1]
    blocks = len(segment_refs) * seg_len // LANES
    lags, times = templ_len // LANES, corr_len // LANES
    tpl = lax.axis_index("tpl")
    for distance, segment_ref in enumerate(segment_refs):
        wave_ref[tpl ^ distance] = segment_ref[...]
    places = [(c * LANES // seg_len, c * LANES % seg_len) for c in range(blocks)]
    block = jnp.concatenate([wave_ref[g, :, at : at + LANES] for g, at in places], axis=0)
    before = jnp.concatenate([jnp.zeros((stations, LANES), jnp.float32), block[:-stations]], axis=0)
    filtered = jnp.dot(
        jnp.concatenate([before, block], axis=1),
        toeplitz_ref[...],
        precision=lax.Precision.HIGHEST,
        preferred_element_type=jnp.float32,
    )
    series = filtered.astype(jnp.bfloat16).astype(jnp.float32)
    series_ref[...] = series
    row = lax.broadcasted_iota(jnp.int32, (LANES, LANES), 0)
    lane = lax.broadcasted_iota(jnp.int32, (LANES, LANES), 1)
    one = jnp.ones((LANES, LANES), jnp.float32)
    sums_of_ref[...] = jnp.concatenate(
        [jnp.where(row <= lane, one, 0.0), jnp.where(row > lane, one, 0.0), one], axis=1
    ).astype(jnp.bfloat16)
    squares = series * series
    high = squares.astype(jnp.bfloat16)
    low = (squares - high.astype(jnp.float32)).astype(jnp.bfloat16)
    sums_ref[...] = jnp.dot(high, sums_of_ref[...], preferred_element_type=jnp.float32) + jnp.dot(
        low, sums_of_ref[...], preferred_element_type=jnp.float32
    )

    def sums(c, kind):
        return sums_ref[c * stations : (c + 1) * stations, kind * LANES : (kind + 1) * LANES]

    for t in range(times):
        energy = sums(t, 0) + sums(t + lags, 1)
        for c in range(t + 1, t + lags):
            energy = energy + sums(c, 2)
        at = (times - 1 - t) * LANES
        inverse_ref[:, at : at + LANES] = lax.rsqrt(energy)
    for s in range(stations):
        whole = jnp.concatenate(
            [series_ref[c * stations + s : c * stations + s + 1, :] for c in reversed(range(blocks))], axis=1
        )
        ahead = pltpu.roll(
            jnp.broadcast_to(whole, (LANES, blocks * LANES)), 0, 1, stride=1, stride_axis=0
        )
        for c in range(1, blocks):
            hankel_ref[s, :, c * LANES : (c + 1) * LANES] = ahead[:, c * LANES : (c + 1) * LANES].astype(jnp.bfloat16)
    me = lax.axis_index("sta") & len(send_refs)
    parts = [me ^ distance for distance in range(1, len(send_refs) + 1)]
    stack_parts(parts, rows_ref, used_ref, shift_ref, hankel_ref, inverse_ref, send_refs)


def keep_kernel(rows_ref, used_ref, shift_ref, hankel_ref, inverse_ref, keep_ref):
    me = lax.axis_index("sta") & (rows_ref.shape[2] - 1)
    stack_parts([me], rows_ref, used_ref, shift_ref, hankel_ref, inverse_ref, [keep_ref])


def flip(value, sta_mask, tpl_mask):
    across = lax.axis_size("tpl")
    mask = sta_mask * across + tpl_mask
    pairs = [(i, i ^ mask) for i in range(lax.axis_size("sta") * across)]
    return lax.ppermute(value, ("sta", "tpl"), pairs)


def shards(waveform, fir_taps, templates, presence, moveout):
    block_rows, stations, templ_len = templates.shape
    owners, segments = lax.axis_size("sta"), lax.axis_size("tpl")
    sta = lax.axis_index("sta")
    samples = segments * waveform.shape[1]
    corr_len = samples - templ_len
    out_len = corr_len - SHIFT_MOST
    owned = block_rows // owners
    parts = min(owners, 4)
    part_rows = block_rows // parts
    vmem = pl.BlockSpec(memory_space=pltpu.VMEM)
    options = dict(
        compiler_params=pltpu.CompilerParams(vmem_limit_bytes=16 * 1024 * 1024),
        cost_estimate=pl.CostEstimate(flops=1 << 20, bytes_accessed=1 << 20, transcendentals=0),
    )
    rows = templates.transpose(1, 0, 2).reshape(stations, owners // parts, parts, owned, templ_len)
    own, toeplitz, used, shift = pl.pallas_call(
        functools.partial(columns_kernel, owners),
        out_shape=(
            jax.ShapeDtypeStruct(waveform.shape, jnp.float32),
            jax.ShapeDtypeStruct((PAIR, LANES), jnp.float32),
            jax.ShapeDtypeStruct((stations, parts, part_rows, LANES), jnp.float32),
            jax.ShapeDtypeStruct((stations, parts, part_rows, LANES), jnp.int32),
        ),
        in_specs=[vmem] * 4,
        out_specs=(vmem,) * 4,
        scratch_shapes=[pltpu.VMEM((8, LANES), jnp.float32)],
        name="columns",
        **options,
    )(waveform, fir_taps[None, :], presence.T, moveout.T)
    sent = {0: waveform}
    bit = segments // 2
    while bit >= 1:
        mask = bit | 1
        for d, piece in list(sent.items()):
            sent[d ^ mask] = flip(piece, 0, mask)
        if bit == segments // 2:
            sent[mask], rows = lax.optimization_barrier((sent[mask], rows))
        bit //= 2
    sent[0] = own
    *send, hankel, inverse = pl.pallas_call(
        functools.partial(send_kernel, segments),
        out_shape=(
            *[jax.ShapeDtypeStruct((owners // parts, owned, out_len), jnp.bfloat16)] * (parts - 1),
            jax.ShapeDtypeStruct((stations, LANES, samples), jnp.bfloat16),
            jax.ShapeDtypeStruct((stations, corr_len), jnp.float32),
        ),
        in_specs=[vmem] * (segments + 4),
        out_specs=(vmem,) * (parts + 1),
        scratch_shapes=[
            pltpu.VMEM((segments,) + waveform.shape, jnp.float32),
            pltpu.VMEM((samples // LANES * stations, LANES), jnp.float32),
            pltpu.VMEM((LANES, 3 * LANES), jnp.bfloat16),
            pltpu.VMEM((samples // LANES * stations, 3 * LANES), jnp.float32),
        ],
        name="send_parts",
        **options,
    )(*[sent[d] for d in range(segments)], toeplitz, rows, used, shift)
    stack = pl.pallas_call(
        keep_kernel,
        out_shape=jax.ShapeDtypeStruct((owners // parts, owned, out_len), jnp.float32),
        in_specs=[vmem] * 5,
        out_specs=vmem,
        name="keep_part",
        **options,
    )(rows, used, shift, hankel, inverse)
    rounds = [parts]
    while rounds[-1] < owners:
        rounds.append(rounds[-1] * 2)
    turns = len(rounds) // 2 * 2 if segments > 1 else 0
    for number, reach in enumerate(rounds):
        turn = 1 if number < turns else 0
        if number == 0:
            moved = [(distance, send[distance - 1]) for distance in range(1, parts)]
        else:
            bit = reach // 2
            pairs = stack.reshape(stack.shape[0] // 2, 2, owned, out_len)
            side = (sta // bit) % 2
            stack = lax.dynamic_index_in_dim(pairs, side, 1, keepdims=False)
            moved = [(bit, lax.dynamic_index_in_dim(pairs, 1 - side, 1, keepdims=False))]
        arrived = [flip(piece, distance, turn) for distance, piece in moved]
        if turn:
            if number == 0:
                stack, _ = lax.optimization_barrier((stack, arrived[-1]))
            if number == 0:
                pieces = [stack[:, :, at : at + LANES] for at in range(0, out_len, LANES)]
                stack = jnp.concatenate([flip(piece, 0, turn) for piece in pieces], axis=2)
            else:
                pieces = [stack[:, : owned // 2], stack[:, owned // 2 :]]
                stack = jnp.concatenate([flip(piece, 0, turn) for piece in pieces], axis=1)
        for piece in arrived:
            stack = stack + piece.astype(jnp.float32)
    return stack


def solution(mesh):
    placed = (P("sta", "tpl"), P(), P("tpl", "sta", None), P("tpl", "sta"), P("tpl", "sta"))
    return jax.shard_map(
        shards, mesh=mesh, in_specs=placed, out_specs=P("tpl", "sta", None), check_vma=False
    )
```

```python
import functools

import jax
import jax.numpy as jnp
from jax import lax
from jax.experimental import pallas as pl
from jax.experimental.pallas import tpu as pltpu
from jax.sharding import PartitionSpec as P

SHIFT_MOST = 128
LANES = 128
PAIR = 2 * LANES
epsilon = 1e-06


def lane_gather(values, index):
    return jnp.take_along_axis(values, index, axis=1, mode="promise_in_bounds")


def as_column(row):
    return jnp.broadcast_to(row, (LANES, row.shape[1])).T


def columns_kernel(owners, wave_in, taps_in, presence_ref, moveout_ref, wave_ref, toeplitz_ref, used_ref, shift_ref, row_ref):
    stations, parts, part_rows, _ = used_ref.shape
    owned = part_rows * parts // owners
    taps = taps_in.shape[1]
    wave_ref[...] = wave_in[...]
    row_ref[...] = jnp.zeros_like(row_ref)
    row_ref[0:1, 0:taps] = taps_in[...]
    sample = lax.broadcasted_iota(jnp.int32, (PAIR, LANES), 0)
    lane = lax.broadcasted_iota(jnp.int32, (PAIR, LANES), 1)
    tap = PAIR - 1 - lane - sample
    picked = lane_gather(jnp.broadcast_to(row_ref[0:1, :], (PAIR, LANES)), tap & (LANES - 1))
    toeplitz_ref[...] = jnp.where((tap >= 0) & (tap < taps), picked, 0.0)
    place = lax.broadcasted_iota(jnp.int32, (LANES, part_rows * parts), 1)
    part, rest = place // part_rows, place % part_rows
    old = (rest // owned * parts + part) * owned + rest % owned
    for s in range(stations):
        shift = lane_gather(jnp.broadcast_to(moveout_ref[s : s + 1, :], old.shape), old)
        shift_ref[s] = shift.T.reshape(shift_ref.shape[1:])
        used = lane_gather(jnp.broadcast_to(presence_ref[s : s + 1, :], old.shape), old)
        used_ref[s] = used.astype(jnp.float32).T.reshape(used_ref.shape[1:])


def stack_parts(parts, rows_ref, used_ref, shift_ref, hankel_ref, inverse_ref, out_refs):
    stations, groups, _, owned, templ_len = rows_ref.shape
    part_rows = groups * owned
    corr_len = inverse_ref.shape[1]
    out_len = out_refs[0].shape[2]
    lag_pairs, time_pairs = templ_len // PAIR, corr_len // PAIR
    total = None
    for s in range(stations):
        rows = jnp.concatenate([rows_ref[s, :, p].reshape(part_rows, templ_len) for p in parts], axis=0)
        raw = [None] * time_pairs
        for offset in reversed(range(1, lag_pairs + time_pairs)):
            uses = [(j, offset - lag_pairs + j) for j in range(lag_pairs) if 0 <= offset - lag_pairs + j < time_pairs]
            at = offset * PAIR
            window = jnp.concatenate(
                [hankel_ref[s, :, at : at + PAIR], hankel_ref[s, :, at - LANES : at - LANES + PAIR]], axis=0
            )
            left = [rows[:, j * PAIR : (j + 1) * PAIR] for j, _ in uses]
            if len(parts) == 1:
                product = jnp.dot(jnp.concatenate(left, axis=0), window, preferred_element_type=jnp.float32)
                made = [product[k * part_rows : (k + 1) * part_rows] for k in range(len(uses))]
            else:
                made = [jnp.dot(values, window, preferred_element_type=jnp.float32) for values in left]
            for (_, t), part in zip(uses, made):
                raw[t] = part if raw[t] is None else raw[t] + part
        inverse = inverse_ref[s : s + 1, :]
        last = corr_len // LANES - 1
        done = []
        for number, p in enumerate(parts):
            first, end = number * part_rows, (number + 1) * part_rows
            wide = rows[first:end].astype(jnp.float32)
            scale = lax.rsqrt(jnp.sum(wide * wide, axis=1, keepdims=True) + epsilon) * used_ref[s, p]
            shift = shift_ref[s, p]
            lane = lax.broadcasted_iota(jnp.int32, shift.shape, 1)
            index = (PAIR - 1 - lane - shift) & (LANES - 1)
            later = lane + shift < LANES
            columns = [
                values[first:end, at : at + LANES] * inverse[:, t * PAIR + at : t * PAIR + at + LANES]
                for t, values in enumerate(raw)
                for at in range(0, PAIR, LANES)
            ]
            done.append(
                [
                    lane_gather(scale * jnp.where(later, columns[last - c], columns[last - 1 - c]), index)
                    for c in range(out_len // LANES)
                ]
            )
        aligned = [jnp.concatenate([part[c] for part in done], axis=0) for c in range(out_len // LANES)]
        total = aligned if total is None else [a + b for a, b in zip(total, aligned)]
    for k, out_ref in enumerate(out_refs):
        for c, part in enumerate(total):
            piece = part[k * part_rows : (k + 1) * part_rows].astype(out_ref.dtype)
            out_ref[:, :, c * LANES : (c + 1) * LANES] = piece.reshape(groups, owned, LANES)


def send_kernel(segments, *refs):
    segment_refs, (toeplitz_ref, rows_ref, used_ref, shift_ref, *send_refs) = refs[:segments], refs[segments:-6]
    hankel_ref, inverse_ref, wave_ref, series_ref, sums_of_ref, sums_ref = refs[-6:]
    stations, templ_len = rows_ref.shape[0], rows_ref.shape[-1]
    corr_len = inverse_ref.shape[1]
    seg_len = segment_refs[0].shape[1]
    blocks = len(segment_refs) * seg_len // LANES
    lags, times = templ_len // LANES, corr_len // LANES
    tpl = lax.axis_index("tpl")
    for distance, segment_ref in enumerate(segment_refs):
        wave_ref[tpl ^ distance] = segment_ref[...]
    places = [(c * LANES // seg_len, c * LANES % seg_len) for c in range(blocks)]
    block = jnp.concatenate([wave_ref[g, :, at : at + LANES] for g, at in places], axis=0)
    before = jnp.concatenate([jnp.zeros((stations, LANES), jnp.float32), block[:-stations]], axis=0)
    filtered = jnp.dot(
        jnp.concatenate([before, block], axis=1),
        toeplitz_ref[...],
        precision=lax.Precision.HIGHEST,
        preferred_element_type=jnp.float32,
    )
    series = filtered.astype(jnp.bfloat16).astype(jnp.float32)
    series_ref[...] = series
    row = lax.broadcasted_iota(jnp.int32, (LANES, LANES), 0)
    lane = lax.broadcasted_iota(jnp.int32, (LANES, LANES), 1)
    one = jnp.ones((LANES, LANES), jnp.float32)
    sums_of_ref[...] = jnp.concatenate(
        [jnp.where(row <= lane, one, 0.0), jnp.where(row > lane, one, 0.0), one], axis=1
    ).astype(jnp.bfloat16)
    squares = series * series
    high = squares.astype(jnp.bfloat16)
    low = (squares - high.astype(jnp.float32)).astype(jnp.bfloat16)
    sums_ref[...] = jnp.dot(high, sums_of_ref[...], preferred_element_type=jnp.float32) + jnp.dot(
        low, sums_of_ref[...], preferred_element_type=jnp.float32
    )

    def sums(c, kind):
        return sums_ref[c * stations : (c + 1) * stations, kind * LANES : (kind + 1) * LANES]

    for t in range(times):
        energy = sums(t, 0) + sums(t + lags, 1)
        for c in range(t + 1, t + lags):
            energy = energy + sums(c, 2)
        at = (times - 1 - t) * LANES
        inverse_ref[:, at : at + LANES] = lax.rsqrt(energy)
    for s in range(stations):
        whole = jnp.concatenate(
            [series_ref[c * stations + s : c * stations + s + 1, :] for c in reversed(range(blocks))], axis=1
        )
        ahead = pltpu.roll(
            jnp.broadcast_to(whole, (LANES, blocks * LANES)), 0, 1, stride=1, stride_axis=0
        )
        for c in range(1, blocks):
            hankel_ref[s, :, c * LANES : (c + 1) * LANES] = ahead[:, c * LANES : (c + 1) * LANES].astype(jnp.bfloat16)
    me = lax.axis_index("sta") & len(send_refs)
    parts = [me ^ distance for distance in range(1, len(send_refs) + 1)]
    stack_parts(parts, rows_ref, used_ref, shift_ref, hankel_ref, inverse_ref, send_refs)


def keep_kernel(rows_ref, used_ref, shift_ref, hankel_ref, inverse_ref, keep_ref):
    me = lax.axis_index("sta") & (rows_ref.shape[2] - 1)
    stack_parts([me], rows_ref, used_ref, shift_ref, hankel_ref, inverse_ref, [keep_ref])


def flip(value, sta_mask, tpl_mask):
    across = lax.axis_size("tpl")
    mask = sta_mask * across + tpl_mask
    pairs = [(i, i ^ mask) for i in range(lax.axis_size("sta") * across)]
    return lax.ppermute(value, ("sta", "tpl"), pairs)


def shards(waveform, fir_taps, templates, presence, moveout):
    block_rows, stations, templ_len = templates.shape
    owners, segments = lax.axis_size("sta"), lax.axis_size("tpl")
    sta = lax.axis_index("sta")
    samples = segments * waveform.shape[1]
    corr_len = samples - templ_len
    out_len = corr_len - SHIFT_MOST
    owned = block_rows // owners
    parts = min(owners, 4)
    part_rows = block_rows // parts
    vmem = pl.BlockSpec(memory_space=pltpu.VMEM)
    options = dict(
        compiler_params=pltpu.CompilerParams(vmem_limit_bytes=16 * 1024 * 1024),
        cost_estimate=pl.CostEstimate(flops=1 << 20, bytes_accessed=1 << 20, transcendentals=0),
    )
    rows = templates.transpose(1, 0, 2).reshape(stations, owners // parts, parts, owned, templ_len)
    own, toeplitz, used, shift = pl.pallas_call(
        functools.partial(columns_kernel, owners),
        out_shape=(
            jax.ShapeDtypeStruct(waveform.shape, jnp.float32),
            jax.ShapeDtypeStruct((PAIR, LANES), jnp.float32),
            jax.ShapeDtypeStruct((stations, parts, part_rows, LANES), jnp.float32),
            jax.ShapeDtypeStruct((stations, parts, part_rows, LANES), jnp.int32),
        ),
        in_specs=[vmem] * 4,
        out_specs=(vmem,) * 4,
        scratch_shapes=[pltpu.VMEM((8, LANES), jnp.float32)],
        name="columns",
        **options,
    )(waveform, fir_taps[None, :], presence.T, moveout.T)
    sent = {0: waveform}
    bit = segments // 2
    while bit >= 1:
        mask = bit | 1
        for d, piece in list(sent.items()):
            sent[d ^ mask] = flip(piece, 0, mask)
        if bit == segments // 2:
            sent[mask], rows = lax.optimization_barrier((sent[mask], rows))
        bit //= 2
    sent[0] = own
    *send, hankel, inverse = pl.pallas_call(
        functools.partial(send_kernel, segments),
        out_shape=(
            *[jax.ShapeDtypeStruct((owners // parts, owned, out_len), jnp.bfloat16)] * (parts - 1),
            jax.ShapeDtypeStruct((stations, LANES, samples), jnp.bfloat16),
            jax.ShapeDtypeStruct((stations, corr_len), jnp.float32),
        ),
        in_specs=[vmem] * (segments + 4),
        out_specs=(vmem,) * (parts + 1),
        scratch_shapes=[
            pltpu.VMEM((segments,) + waveform.shape, jnp.float32),
            pltpu.VMEM((samples // LANES * stations, LANES), jnp.float32),
            pltpu.VMEM((LANES, 3 * LANES), jnp.bfloat16),
            pltpu.VMEM((samples // LANES * stations, 3 * LANES), jnp.float32),
        ],
        name="send_parts",
        **options,
    )(*[sent[d] for d in range(segments)], toeplitz, rows, used, shift)
    stack = pl.pallas_call(
        keep_kernel,
        out_shape=jax.ShapeDtypeStruct((owners // parts, owned, out_len), jnp.float32),
        in_specs=[vmem] * 5,
        out_specs=vmem,
        name="keep_part",
        **options,
    )(rows, used, shift, hankel, inverse)
    rounds = [parts]
    while rounds[-1] < owners:
        rounds.append(rounds[-1] * 2)
    turns = len(rounds) // 2 * 2 if segments > 1 else 0
    for number, reach in enumerate(rounds):
        turn = 1 if number < turns else 0
        if number == 0:
            moved = [(distance, send[distance - 1]) for distance in range(1, parts)]
        else:
            bit = reach // 2
            pairs = stack.reshape(stack.shape[0] // 2, 2, owned, out_len)
            side = (sta // bit) % 2
            stack = lax.dynamic_index_in_dim(pairs, side, 1, keepdims=False)
            moved = [(bit, lax.dynamic_index_in_dim(pairs, 1 - side, 1, keepdims=False))]
        arrived = [flip(piece, distance, turn) for distance, piece in moved]
        if turn:
            if number == 0:
                stack, _ = lax.optimization_barrier((stack, arrived[-1]))
            if number == 0:
                pieces = [stack[:, :, at : at + LANES] for at in range(0, out_len, LANES)]
                stack = jnp.concatenate([flip(piece, 0, turn) for piece in pieces], axis=2)
            else:
                pieces = [stack[:, : owned // 2], stack[:, owned // 2 :]]
                stack = jnp.concatenate([flip(piece, 0, turn) for piece in pieces], axis=1)
        for piece in arrived:
            stack = stack + piece.astype(jnp.float32)
    return stack


def solution(mesh):
    placed = (P("sta", "tpl"), P(), P("tpl", "sta", None), P("tpl", "sta"), P("tpl", "sta"))
    return jax.shard_map(
        shards, mesh=mesh, in_specs=placed, out_specs=P("tpl", "sta", None), check_vma=False
    )
```

```python
import functools

import jax
import jax.numpy as jnp
from jax import lax
from jax.experimental import pallas as pl
from jax.experimental.pallas import tpu as pltpu
from jax.sharding import PartitionSpec as P

SHIFT_MOST = 128
LANES = 128
PAIR = 2 * LANES
epsilon = 1e-06


def lane_gather(values, index):
    return jnp.take_along_axis(values, index, axis=1, mode="promise_in_bounds")


def as_column(row):
    return jnp.broadcast_to(row, (LANES, row.shape[1])).T


def columns_kernel(owners, wave_in, taps_in, presence_ref, moveout_ref, wave_ref, toeplitz_ref, used_ref, shift_ref, row_ref):
    stations, parts, part_rows, _ = used_ref.shape
    owned = part_rows * parts // owners
    taps = taps_in.shape[1]
    wave_ref[...] = wave_in[...]
    row_ref[...] = jnp.zeros_like(row_ref)
    row_ref[0:1, 0:taps] = taps_in[...]
    sample = lax.broadcasted_iota(jnp.int32, (PAIR, LANES), 0)
    lane = lax.broadcasted_iota(jnp.int32, (PAIR, LANES), 1)
    tap = PAIR - 1 - lane - sample
    picked = lane_gather(jnp.broadcast_to(row_ref[0:1, :], (PAIR, LANES)), tap & (LANES - 1))
    toeplitz_ref[...] = jnp.where((tap >= 0) & (tap < taps), picked, 0.0)
    place = lax.broadcasted_iota(jnp.int32, (LANES, part_rows * parts), 1)
    part, rest = place // part_rows, place % part_rows
    old = (rest // owned * parts + part) * owned + rest % owned
    for s in range(stations):
        shift = lane_gather(jnp.broadcast_to(moveout_ref[s : s + 1, :], old.shape), old)
        shift_ref[s] = shift.T.reshape(shift_ref.shape[1:])
        used = lane_gather(jnp.broadcast_to(presence_ref[s : s + 1, :], old.shape), old)
        used_ref[s] = used.astype(jnp.float32).T.reshape(used_ref.shape[1:])


def stack_parts(parts, rows_ref, used_ref, shift_ref, hankel_ref, inverse_ref, out_refs):
    stations, groups, _, owned, templ_len = rows_ref.shape
    part_rows = groups * owned
    corr_len = inverse_ref.shape[1]
    out_len = out_refs[0].shape[2]
    lag_pairs, time_pairs = templ_len // PAIR, corr_len // PAIR
    total = None
    for s in range(stations):
        rows = jnp.concatenate([rows_ref[s, :, p].reshape(part_rows, templ_len) for p in parts], axis=0)
        raw = [None] * time_pairs
        for offset in reversed(range(1, lag_pairs + time_pairs)):
            uses = [(j, offset - lag_pairs + j) for j in range(lag_pairs) if 0 <= offset - lag_pairs + j < time_pairs]
            at = offset * PAIR
            window = jnp.concatenate(
                [hankel_ref[s, :, at : at + PAIR], hankel_ref[s, :, at - LANES : at - LANES + PAIR]], axis=0
            )
            left = [rows[:, j * PAIR : (j + 1) * PAIR] for j, _ in uses]
            if len(parts) == 1:
                product = jnp.dot(jnp.concatenate(left, axis=0), window, preferred_element_type=jnp.float32)
                made = [product[k * part_rows : (k + 1) * part_rows] for k in range(len(uses))]
            else:
                made = [jnp.dot(values, window, preferred_element_type=jnp.float32) for values in left]
            for (_, t), part in zip(uses, made):
                raw[t] = part if raw[t] is None else raw[t] + part
        inverse = inverse_ref[s : s + 1, :]
        last = corr_len // LANES - 1
        done = []
        for number, p in enumerate(parts):
            first, end = number * part_rows, (number + 1) * part_rows
            wide = rows[first:end].astype(jnp.float32)
            scale = lax.rsqrt(jnp.sum(wide * wide, axis=1, keepdims=True) + epsilon) * used_ref[s, p]
            shift = shift_ref[s, p]
            lane = lax.broadcasted_iota(jnp.int32, shift.shape, 1)
            index = (PAIR - 1 - lane - shift) & (LANES - 1)
            later = lane + shift < LANES
            columns = [
                values[first:end, at : at + LANES] * inverse[:, t * PAIR + at : t * PAIR + at + LANES]
                for t, values in enumerate(raw)
                for at in range(0, PAIR, LANES)
            ]
            done.append(
                [
                    lane_gather(scale * jnp.where(later, columns[last - c], columns[last - 1 - c]), index)
                    for c in range(out_len // LANES)
                ]
            )
        aligned = [jnp.concatenate([part[c] for part in done], axis=0) for c in range(out_len // LANES)]
        total = aligned if total is None else [a + b for a, b in zip(total, aligned)]
    for k, out_ref in enumerate(out_refs):
        for c, part in enumerate(total):
            piece = part[k * part_rows : (k + 1) * part_rows].astype(out_ref.dtype)
            out_ref[:, :, c * LANES : (c + 1) * LANES] = piece.reshape(groups, owned, LANES)


def send_kernel(segments, *refs):
    segment_refs, (toeplitz_ref, rows_ref, used_ref, shift_ref, *send_refs) = refs[:segments], refs[segments:-6]
    hankel_ref, inverse_ref, wave_ref, series_ref, sums_of_ref, sums_ref = refs[-6:]
    stations, templ_len = rows_ref.shape[0], rows_ref.shape[-1]
    corr_len = inverse_ref.shape[1]
    seg_len = segment_refs[0].shape[1]
    blocks = len(segment_refs) * seg_len // LANES
    lags, times = templ_len // LANES, corr_len // LANES
    tpl = lax.axis_index("tpl")
    for distance, segment_ref in enumerate(segment_refs):
        wave_ref[tpl ^ distance] = segment_ref[...]
    places = [(c * LANES // seg_len, c * LANES % seg_len) for c in range(blocks)]
    block = jnp.concatenate([wave_ref[g, :, at : at + LANES] for g, at in places], axis=0)
    before = jnp.concatenate([jnp.zeros((stations, LANES), jnp.float32), block[:-stations]], axis=0)
    filtered = jnp.dot(
        jnp.concatenate([before, block], axis=1),
        toeplitz_ref[...],
        precision=lax.Precision.HIGHEST,
        preferred_element_type=jnp.float32,
    )
    series = filtered.astype(jnp.bfloat16).astype(jnp.float32)
    series_ref[...] = series
    row = lax.broadcasted_iota(jnp.int32, (LANES, LANES), 0)
    lane = lax.broadcasted_iota(jnp.int32, (LANES, LANES), 1)
    one = jnp.ones((LANES, LANES), jnp.float32)
    sums_of_ref[...] = jnp.concatenate(
        [jnp.where(row <= lane, one, 0.0), jnp.where(row > lane, one, 0.0), one], axis=1
    ).astype(jnp.bfloat16)
    squares = series * series
    high = squares.astype(jnp.bfloat16)
    low = (squares - high.astype(jnp.float32)).astype(jnp.bfloat16)
    sums_ref[...] = jnp.dot(high, sums_of_ref[...], preferred_element_type=jnp.float32) + jnp.dot(
        low, sums_of_ref[...], preferred_element_type=jnp.float32
    )

    def sums(c, kind):
        return sums_ref[c * stations : (c + 1) * stations, kind * LANES : (kind + 1) * LANES]

    for t in range(times):
        energy = sums(t, 0) + sums(t + lags, 1)
        for c in range(t + 1, t + lags):
            energy = energy + sums(c, 2)
        at = (times - 1 - t) * LANES
        inverse_ref[:, at : at + LANES] = lax.rsqrt(energy)
    for s in range(stations):
        whole = jnp.concatenate(
            [series_ref[c * stations + s : c * stations + s + 1, :] for c in reversed(range(blocks))], axis=1
        )
        ahead = pltpu.roll(
            jnp.broadcast_to(whole, (LANES, blocks * LANES)), 0, 1, stride=1, stride_axis=0
        )
        for c in reversed(range(1, blocks)):
            hankel_ref[s, :, c * LANES : (c + 1) * LANES] = ahead[:, c * LANES : (c + 1) * LANES].astype(jnp.bfloat16)
    me = lax.axis_index("sta") & len(send_refs)
    parts = [me ^ distance for distance in range(1, len(send_refs) + 1)]
    stack_parts(parts, rows_ref, used_ref, shift_ref, hankel_ref, inverse_ref, send_refs)


def keep_kernel(rows_ref, used_ref, shift_ref, hankel_ref, inverse_ref, keep_ref):
    me = lax.axis_index("sta") & (rows_ref.shape[2] - 1)
    stack_parts([me], rows_ref, used_ref, shift_ref, hankel_ref, inverse_ref, [keep_ref])


def flip(value, sta_mask, tpl_mask):
    across = lax.axis_size("tpl")
    mask = sta_mask * across + tpl_mask
    pairs = [(i, i ^ mask) for i in range(lax.axis_size("sta") * across)]
    return lax.ppermute(value, ("sta", "tpl"), pairs)


def shards(waveform, fir_taps, templates, presence, moveout):
    block_rows, stations, templ_len = templates.shape
    owners, segments = lax.axis_size("sta"), lax.axis_size("tpl")
    sta = lax.axis_index("sta")
    samples = segments * waveform.shape[1]
    corr_len = samples - templ_len
    out_len = corr_len - SHIFT_MOST
    owned = block_rows // owners
    parts = min(owners, 4)
    part_rows = block_rows // parts
    vmem = pl.BlockSpec(memory_space=pltpu.VMEM)
    options = dict(
        compiler_params=pltpu.CompilerParams(vmem_limit_bytes=16 * 1024 * 1024),
        cost_estimate=pl.CostEstimate(flops=1 << 20, bytes_accessed=1 << 20, transcendentals=0),
    )
    rows = templates.transpose(1, 0, 2).reshape(stations, owners // parts, parts, owned, templ_len)
    own, toeplitz, used, shift = pl.pallas_call(
        functools.partial(columns_kernel, owners),
        out_shape=(
            jax.ShapeDtypeStruct(waveform.shape, jnp.float32),
            jax.ShapeDtypeStruct((PAIR, LANES), jnp.float32),
            jax.ShapeDtypeStruct((stations, parts, part_rows, LANES), jnp.float32),
            jax.ShapeDtypeStruct((stations, parts, part_rows, LANES), jnp.int32),
        ),
        in_specs=[vmem] * 4,
        out_specs=(vmem,) * 4,
        scratch_shapes=[pltpu.VMEM((8, LANES), jnp.float32)],
        name="columns",
        **options,
    )(waveform, fir_taps[None, :], presence.T, moveout.T)
    sent = {0: waveform}
    bit = segments // 2
    while bit >= 1:
        mask = bit | 1
        for d, piece in list(sent.items()):
            sent[d ^ mask] = flip(piece, 0, mask)
        if bit == segments // 2:
            sent[mask], rows = lax.optimization_barrier((sent[mask], rows))
        bit //= 2
    sent[0] = own
    *send, hankel, inverse = pl.pallas_call(
        functools.partial(send_kernel, segments),
        out_shape=(
            *[jax.ShapeDtypeStruct((owners // parts, owned, out_len), jnp.bfloat16)] * (parts - 1),
            jax.ShapeDtypeStruct((stations, LANES, samples), jnp.bfloat16),
            jax.ShapeDtypeStruct((stations, corr_len), jnp.float32),
        ),
        in_specs=[vmem] * (segments + 4),
        out_specs=(vmem,) * (parts + 1),
        scratch_shapes=[
            pltpu.VMEM((segments,) + waveform.shape, jnp.float32),
            pltpu.VMEM((samples // LANES * stations, LANES), jnp.float32),
            pltpu.VMEM((LANES, 3 * LANES), jnp.bfloat16),
            pltpu.VMEM((samples // LANES * stations, 3 * LANES), jnp.float32),
        ],
        name="send_parts",
        **options,
    )(*[sent[d] for d in range(segments)], toeplitz, rows, used, shift)
    stack = pl.pallas_call(
        keep_kernel,
        out_shape=jax.ShapeDtypeStruct((owners // parts, owned, out_len), jnp.float32),
        in_specs=[vmem] * 5,
        out_specs=vmem,
        name="keep_part",
        **options,
    )(rows, used, shift, hankel, inverse)
    rounds = [parts]
    while rounds[-1] < owners:
        rounds.append(rounds[-1] * 2)
    turns = len(rounds) // 2 * 2 if segments > 1 else 0
    for number, reach in enumerate(rounds):
        turn = 1 if number < turns else 0
        if number == 0:
            moved = [(distance, send[distance - 1]) for distance in range(1, parts)]
        else:
            bit = reach // 2
            pairs = stack.reshape(stack.shape[0] // 2, 2, owned, out_len)
            side = (sta // bit) % 2
            stack = lax.dynamic_index_in_dim(pairs, side, 1, keepdims=False)
            moved = [(bit, lax.dynamic_index_in_dim(pairs, 1 - side, 1, keepdims=False))]
        arrived = [flip(piece, distance, turn) for distance, piece in moved]
        if turn:
            if number == 0:
                stack, _ = lax.optimization_barrier((stack, arrived[-1]))
            if number == 0:
                pieces = [stack[:, :, at : at + LANES] for at in range(0, out_len, LANES)]
                stack = jnp.concatenate([flip(piece, 0, turn) for piece in pieces], axis=2)
            else:
                pieces = [stack[:, : owned // 2], stack[:, owned // 2 :]]
                stack = jnp.concatenate([flip(piece, 0, turn) for piece in pieces], axis=1)
        for piece in arrived:
            stack = stack + piece.astype(jnp.float32)
    return stack


def solution(mesh):
    placed = (P("sta", "tpl"), P(), P("tpl", "sta", None), P("tpl", "sta"), P("tpl", "sta"))
    return jax.shard_map(
        shards, mesh=mesh, in_specs=placed, out_specs=P("tpl", "sta", None), check_vma=False
    )
```

```python
import functools

import jax
import jax.numpy as jnp
from jax import lax
from jax.experimental import pallas as pl
from jax.experimental.pallas import tpu as pltpu
from jax.sharding import PartitionSpec as P

SHIFT_MOST = 128
LANES = 128
PAIR = 2 * LANES
epsilon = 1e-06


def lane_gather(values, index):
    return jnp.take_along_axis(values, index, axis=1, mode="promise_in_bounds")


def as_column(row):
    return jnp.broadcast_to(row, (LANES, row.shape[1])).T


def columns_kernel(owners, wave_in, taps_in, presence_ref, moveout_ref, wave_ref, toeplitz_ref, used_ref, shift_ref, row_ref):
    stations, parts, part_rows, _ = used_ref.shape
    owned = part_rows * parts // owners
    taps = taps_in.shape[1]
    wave_ref[...] = wave_in[...]
    row_ref[...] = jnp.zeros_like(row_ref)
    row_ref[0:1, 0:taps] = taps_in[...]
    sample = lax.broadcasted_iota(jnp.int32, (PAIR, LANES), 0)
    lane = lax.broadcasted_iota(jnp.int32, (PAIR, LANES), 1)
    tap = PAIR - 1 - lane - sample
    picked = lane_gather(jnp.broadcast_to(row_ref[0:1, :], (PAIR, LANES)), tap & (LANES - 1))
    toeplitz_ref[...] = jnp.where((tap >= 0) & (tap < taps), picked, 0.0)
    place = lax.broadcasted_iota(jnp.int32, (LANES, part_rows * parts), 1)
    part, rest = place // part_rows, place % part_rows
    old = (rest // owned * parts + part) * owned + rest % owned
    for s in range(stations):
        shift = lane_gather(jnp.broadcast_to(moveout_ref[s : s + 1, :], old.shape), old)
        shift_ref[s] = shift.T.reshape(shift_ref.shape[1:])
        used = lane_gather(jnp.broadcast_to(presence_ref[s : s + 1, :], old.shape), old)
        used_ref[s] = used.astype(jnp.float32).T.reshape(used_ref.shape[1:])


def stack_parts(parts, rows_ref, used_ref, shift_ref, hankel_ref, inverse_ref, out_refs):
    stations, groups, _, owned, templ_len = rows_ref.shape
    part_rows = groups * owned
    corr_len = inverse_ref.shape[1]
    out_len = out_refs[0].shape[2]
    lag_pairs, time_pairs = templ_len // PAIR, corr_len // PAIR
    total = None
    for s in range(stations):
        rows = jnp.concatenate([rows_ref[s, :, p].reshape(part_rows, templ_len) for p in parts], axis=0)
        raw = [None] * time_pairs
        for offset in reversed(range(1, lag_pairs + time_pairs)):
            uses = [(j, offset - lag_pairs + j) for j in range(lag_pairs) if 0 <= offset - lag_pairs + j < time_pairs]
            at = offset * PAIR
            window = jnp.concatenate(
                [hankel_ref[s, :, at : at + PAIR], hankel_ref[s, :, at - LANES : at - LANES + PAIR]], axis=0
            )
            left = [rows[:, j * PAIR : (j + 1) * PAIR] for j, _ in uses]
            if len(parts) == 1:
                product = jnp.dot(jnp.concatenate(left, axis=0), window, preferred_element_type=jnp.float32)
                made = [product[k * part_rows : (k + 1) * part_rows] for k in range(len(uses))]
            else:
                made = [jnp.dot(values, window, preferred_element_type=jnp.float32) for values in left]
            for (_, t), part in zip(uses, made):
                raw[t] = part if raw[t] is None else raw[t] + part
        inverse = inverse_ref[s : s + 1, :]
        last = corr_len // LANES - 1
        done = []
        for number, p in enumerate(parts):
            first, end = number * part_rows, (number + 1) * part_rows
            wide = rows[first:end].astype(jnp.float32)
            scale = lax.rsqrt(jnp.sum(wide * wide, axis=1, keepdims=True) + epsilon) * used_ref[s, p]
            shift = shift_ref[s, p]
            lane = lax.broadcasted_iota(jnp.int32, shift.shape, 1)
            index = (PAIR - 1 - lane - shift) & (LANES - 1)
            later = lane + shift < LANES
            columns = [
                values[first:end, at : at + LANES] * inverse[:, t * PAIR + at : t * PAIR + at + LANES]
                for t, values in enumerate(raw)
                for at in range(0, PAIR, LANES)
            ]
            done.append(
                [
                    lane_gather(scale * jnp.where(later, columns[last - c], columns[last - 1 - c]), index)
                    for c in range(out_len // LANES)
                ]
            )
        aligned = [jnp.concatenate([part[c] for part in done], axis=0) for c in range(out_len // LANES)]
        total = aligned if total is None else [a + b for a, b in zip(total, aligned)]
    for k, out_ref in enumerate(out_refs):
        for c, part in enumerate(total):
            piece = part[k * part_rows : (k + 1) * part_rows].astype(out_ref.dtype)
            out_ref[:, :, c * LANES : (c + 1) * LANES] = piece.reshape(groups, owned, LANES)


def send_kernel(segments, *refs):
    segment_refs, (toeplitz_ref, rows_ref, used_ref, shift_ref, *send_refs) = refs[:segments], refs[segments:-6]
    hankel_ref, inverse_ref, wave_ref, series_ref, sums_of_ref, sums_ref = refs[-6:]
    stations, templ_len = rows_ref.shape[0], rows_ref.shape[-1]
    corr_len = inverse_ref.shape[1]
    seg_len = segment_refs[0].shape[1]
    blocks = len(segment_refs) * seg_len // LANES
    lags, times = templ_len // LANES, corr_len // LANES
    tpl = lax.axis_index("tpl")
    for distance, segment_ref in enumerate(segment_refs):
        wave_ref[tpl ^ distance] = segment_ref[...]
    places = [(c * LANES // seg_len, c * LANES % seg_len) for c in range(blocks)]
    block = jnp.concatenate([wave_ref[g, :, at : at + LANES] for g, at in places], axis=0)
    before = jnp.concatenate([jnp.zeros((stations, LANES), jnp.float32), block[:-stations]], axis=0)
    filtered = jnp.dot(
        jnp.concatenate([before, block], axis=1),
        toeplitz_ref[...],
        precision=lax.Precision.HIGHEST,
        preferred_element_type=jnp.float32,
    )
    series = filtered.astype(jnp.bfloat16).astype(jnp.float32)
    series_ref[...] = series
    row = lax.broadcasted_iota(jnp.int32, (LANES, LANES), 0)
    lane = lax.broadcasted_iota(jnp.int32, (LANES, LANES), 1)
    one = jnp.ones((LANES, LANES), jnp.float32)
    sums_of_ref[...] = jnp.concatenate(
        [jnp.where(row <= lane, one, 0.0), jnp.where(row > lane, one, 0.0), one], axis=1
    ).astype(jnp.bfloat16)
    squares = series * series
    high = squares.astype(jnp.bfloat16)
    low = (squares - high.astype(jnp.float32)).astype(jnp.bfloat16)
    sums_ref[...] = jnp.dot(high, sums_of_ref[...], preferred_element_type=jnp.float32) + jnp.dot(
        low, sums_of_ref[...], preferred_element_type=jnp.float32
    )

    def sums(c, kind):
        return sums_ref[c * stations : (c + 1) * stations, kind * LANES : (kind + 1) * LANES]

    for t in range(times):
        energy = sums(t, 0) + sums(t + lags, 1)
        for c in range(t + 1, t + lags):
            energy = energy + sums(c, 2)
        at = (times - 1 - t) * LANES
        inverse_ref[:, at : at + LANES] = lax.rsqrt(energy)
    for s in range(stations):
        whole = jnp.concatenate(
            [series_ref[c * stations + s : c * stations + s + 1, :] for c in reversed(range(blocks))], axis=1
        )
        ahead = pltpu.roll(
            jnp.broadcast_to(whole, (LANES, blocks * LANES)), 0, 1, stride=1, stride_axis=0
        )
        for c in range(1, blocks):
            hankel_ref[s, :, c * LANES : (c + 1) * LANES] = ahead[:, c * LANES : (c + 1) * LANES].astype(jnp.bfloat16)
    me = lax.axis_index("sta") & len(send_refs)
    parts = [me ^ distance for distance in range(1, len(send_refs) + 1)]
    stack_parts(parts, rows_ref, used_ref, shift_ref, hankel_ref, inverse_ref, send_refs)


def keep_kernel(rows_ref, used_ref, shift_ref, hankel_ref, inverse_ref, keep_ref):
    me = lax.axis_index("sta") & (rows_ref.shape[2] - 1)
    stack_parts([me], rows_ref, used_ref, shift_ref, hankel_ref, inverse_ref, [keep_ref])


def flip(value, sta_mask, tpl_mask):
    across = lax.axis_size("tpl")
    mask = sta_mask * across + tpl_mask
    pairs = [(i, i ^ mask) for i in range(lax.axis_size("sta") * across)]
    return lax.ppermute(value, ("sta", "tpl"), pairs)


def shards(waveform, fir_taps, templates, presence, moveout):
    block_rows, stations, templ_len = templates.shape
    owners, segments = lax.axis_size("sta"), lax.axis_size("tpl")
    sta = lax.axis_index("sta")
    samples = segments * waveform.shape[1]
    corr_len = samples - templ_len
    out_len = corr_len - SHIFT_MOST
    owned = block_rows // owners
    parts = min(owners, 4)
    part_rows = block_rows // parts
    vmem = pl.BlockSpec(memory_space=pltpu.VMEM)
    options = dict(
        compiler_params=pltpu.CompilerParams(vmem_limit_bytes=16 * 1024 * 1024),
        cost_estimate=pl.CostEstimate(flops=1 << 20, bytes_accessed=1 << 20, transcendentals=0),
    )
    rows = templates.transpose(1, 0, 2).reshape(stations, owners // parts, parts, owned, templ_len)
    own, toeplitz, used, shift = pl.pallas_call(
        functools.partial(columns_kernel, owners),
        out_shape=(
            jax.ShapeDtypeStruct(waveform.shape, jnp.float32),
            jax.ShapeDtypeStruct((PAIR, LANES), jnp.float32),
            jax.ShapeDtypeStruct((stations, parts, part_rows, LANES), jnp.float32),
            jax.ShapeDtypeStruct((stations, parts, part_rows, LANES), jnp.int32),
        ),
        in_specs=[vmem] * 4,
        out_specs=(vmem,) * 4,
        scratch_shapes=[pltpu.VMEM((8, LANES), jnp.float32)],
        name="columns",
        **options,
    )(waveform, fir_taps[None, :], presence.T, moveout.T)
    sent = {0: waveform}
    bit = segments // 2
    while bit >= 1:
        mask = bit | 1
        for d, piece in list(sent.items()):
            sent[d ^ mask] = flip(piece, 0, mask)
        if bit == segments // 2:
            sent[mask], rows = lax.optimization_barrier((sent[mask], rows))
        bit //= 2
    sent[0] = own
    *send, hankel, inverse = pl.pallas_call(
        functools.partial(send_kernel, segments),
        out_shape=(
            *[jax.ShapeDtypeStruct((owners // parts, owned, out_len), jnp.bfloat16)] * (parts - 1),
            jax.ShapeDtypeStruct((stations, LANES, samples), jnp.bfloat16),
            jax.ShapeDtypeStruct((stations, corr_len), jnp.float32),
        ),
        in_specs=[vmem] * (segments + 4),
        out_specs=(vmem,) * (parts + 1),
        scratch_shapes=[
            pltpu.VMEM((segments,) + waveform.shape, jnp.float32),
            pltpu.VMEM((samples // LANES * stations, LANES), jnp.float32),
            pltpu.VMEM((LANES, 3 * LANES), jnp.bfloat16),
            pltpu.VMEM((samples // LANES * stations, 3 * LANES), jnp.float32),
        ],
        name="send_parts",
        **options,
    )(*[sent[d] for d in range(segments)], toeplitz, rows, used, shift)
    stack = pl.pallas_call(
        keep_kernel,
        out_shape=jax.ShapeDtypeStruct((owners // parts, owned, out_len), jnp.float32),
        in_specs=[vmem] * 5,
        out_specs=vmem,
        name="keep_part",
        **options,
    )(rows, used, shift, hankel, inverse)
    rounds = [parts]
    while rounds[-1] < owners:
        rounds.append(rounds[-1] * 2)
    turns = len(rounds) // 2 * 2 if segments > 1 else 0
    for number, reach in enumerate(rounds):
        turn = 1 if number < turns else 0
        if number == 0:
            moved = [(distance, send[distance - 1]) for distance in (*range(parts - 2, 0, -1), parts - 1)]
        else:
            bit = reach // 2
            pairs = stack.reshape(stack.shape[0] // 2, 2, owned, out_len)
            side = (sta // bit) % 2
            stack = lax.dynamic_index_in_dim(pairs, side, 1, keepdims=False)
            moved = [(bit, lax.dynamic_index_in_dim(pairs, 1 - side, 1, keepdims=False))]
        arrived = [flip(piece, distance, turn) for distance, piece in moved]
        if turn:
            if number == 0:
                stack, _ = lax.optimization_barrier((stack, arrived[-1]))
            if number == 0:
                pieces = [stack[:, :, at : at + LANES] for at in range(0, out_len, LANES)]
                stack = jnp.concatenate([flip(piece, 0, turn) for piece in pieces], axis=2)
            else:
                pieces = [stack[:, : owned // 2], stack[:, owned // 2 :]]
                stack = jnp.concatenate([flip(piece, 0, turn) for piece in pieces], axis=1)
        for piece in arrived:
            stack = stack + piece.astype(jnp.float32)
    return stack


def solution(mesh):
    placed = (P("sta", "tpl"), P(), P("tpl", "sta", None), P("tpl", "sta"), P("tpl", "sta"))
    return jax.shard_map(
        shards, mesh=mesh, in_specs=placed, out_specs=P("tpl", "sta", None), check_vma=False
    )
```
